32 devices in a mesh: seq: 8 (over y, x, core), head: 4 (over z).
Axes of the slice: x: 2, y: 2, z: 4, core: 2. Of those that a mesh axis runs over, the one named last changes fastest.
Arguments:
- tokens: bfloat16 [65536, 512], P(('seq', 'head')), may hold values from -6 to 6
- seq_lengths: int32 [8, 16], P('seq'), may hold values from 0 to 1024, as said below
- ln1_gain: float32 [512], replicated, may hold values from 0.5 to 1.5
- ln1_bias: float32 [512], replicated, may hold values from -3 to 3
- w_qkv: bfloat16 [512, 1536], replicated, may hold values from -0.375 to 0.375
- w_out: bfloat16 [512, 512], replicated, may hold values from -1 to 1
- w_gate1: bfloat16 [512, 512], replicated, may hold values from -0.25 to 0.25
- gate1_gain: float32 [512], replicated, may hold values from 0.5 to 2
- gate1_shift: float32 [512], replicated, may hold values from -3 to 3
- ln2_gain: float32 [512], replicated, may hold values from 0.5 to 1.5
- ln2_bias: float32 [512], replicated, may hold values from -3 to 3
- w_up: bfloat16 [512, 2048], replicated, may hold values from -0.25 to 0.25
- b_up: float32 [2048], replicated, may hold values from -3 to 3
- w_down: bfloat16 [2048, 512], replicated, may hold values from -0.1875 to 0.1875
- b_down: float32 [512], replicated, may hold values from -3 to 3
- w_gate2: bfloat16 [512, 512], replicated, may hold values from -0.25 to 0.25
- gate2_gain: float32 [512], replicated, may hold values from 0.5 to 2
- gate2_shift: float32 [512], replicated, may hold values from -3 to 3
- cotangent: bfloat16 [65536, 512], P(('seq', 'head')), may hold values from -6 to 6
Outputs:
- output: bfloat16 [65536, 512], P(('seq', 'head'))
- grad_tokens: float32 [65536, 512], P(('seq', 'head'))
- g_ln1_gain: float32 [512], replicated
- g_ln1_bias: float32 [512], replicated
- g_w_qkv: float32 [512, 1536], replicated
- g_w_out: float32 [512, 512], replicated
- g_w_gate1: float32 [512, 512], replicated
- g_gate1_gain: float32 [512], replicated
- g_gate1_shift: float32 [512], replicated
- g_ln2_gain: float32 [512], replicated
- g_ln2_bias: float32 [512], replicated
- g_w_up: float32 [512, 2048], replicated
- g_b_up: float32 [2048], replicated
- g_w_down: float32 [2048, 512], replicated
- g_b_down: float32 [512], replicated
- g_w_gate2: float32 [512, 512], replicated
- g_gate2_gain: float32 [512], replicated
- g_gate2_shift: float32 [512], replicated
The draws below stay inside these ranges and needn't reach their ends.
Inputs may be any that keep to these rules, and one draw needn't show every extreme that they name: `seq_lengths`: each row lists the lengths of its group's sequences in order, each 512 or 1024, the two lengths mixed in any order within a group, followed by zeros; each row sums to 8192.
All inputs are finite; a program needn't handle non-finite values.
Results may differ from the reference program's by a relative error of at most 0.013.
The reference program's roundings to bfloat16 on the way count: a program that leaves them out, or rounds other values in their place, can miss the bound.
Values may be sent and summed in bfloat16 or wider, within the bound.
No kernel may reach another device: no remote copies, remote signals or barrier semaphores. Data moves between devices by JAX's collectives and lax.ppermute only.
A program may use at most 256 MiB of HBM per device.

```python
import math
import jax
import jax.numpy as jnp
from jax import lax

D = 512
HEADS = 8
HD = 64
FF = 2048
SHORT = 512
SLOTS = 16
GROUPS = 8
TOKENS = 65536


def draw_seq_lengths(key, part):
    key = jax.random.fold_in(key, 11)
    count_key, order_key = jax.random.split(key)
    longs = jax.random.randint(count_key, (GROUPS,), 0, SLOTS // 2 + 1)
    place = jnp.arange(GROUPS)
    longs = jnp.where(place == 0, SLOTS // 2, jnp.where(place == GROUPS - 1, 0, longs))
    items = SLOTS - longs
    ranks = jax.vmap(lambda sub: jax.random.permutation(sub, SLOTS))(jax.random.split(order_key, GROUPS))
    column = jnp.arange(SLOTS)
    valid = column[None, :] < items[:, None]
    before = valid[:, None, :] & (ranks[:, None, :] < ranks[:, :, None])
    order = jnp.sum(before.astype(jnp.int32), axis=2)
    is_long = order < longs[:, None]
    return jnp.where(valid, jnp.where(is_long, 2 * SHORT, SHORT), 0).astype(jnp.int32)


def block_scale(rng, dims, shards, low, top_value):
    level, own = 1.0, jax.random.fold_in(rng, 6)
    for position, parts in shards:
        draws = jnp.exp(jax.random.uniform(jax.random.fold_in(own, position), (parts,), jnp.float32, low / len(shards), top_value / len(shards)))
        level = level * jnp.repeat(draws, dims[position] // parts).reshape([-1 if axis == position else 1 for axis in range(len(dims))])
    return level


def gaussian(stream_key, dims, width, reach, pieces=(), held_as=jnp.bfloat16):
    level = block_scale(stream_key, dims, pieces, -0.22, 0.18) if pieces else 1.0
    array = jax.random.normal(stream_key, dims, jnp.float32) * width * level
    return jnp.minimum(jnp.maximum(array, -reach), reach).astype(held_as)


def setup_inputs(seed: int = 0) -> dict:
    splits = jax.random.split(jax.random.key(seed), 20)
    return {
        "tokens": gaussian(splits[0], (TOKENS, D), 1.0, 6.0, ((0, 32),)),
        "seq_lengths": draw_seq_lengths(jax.random.fold_in(splits[19], 71), 0),
        "ln1_gain": jnp.clip(1.0 + 0.1 * jax.random.normal(splits[2], (D,), jnp.float32), 0.5, 1.5),
        "ln1_bias": gaussian(splits[3], (D,), 0.5, 3.0, (), jnp.float32),
        "w_qkv": gaussian(splits[4], (D, 3 * D), (D // 2) ** -0.5, 0.375),
        "w_out": gaussian(splits[5], (D, D), (D // 16) ** -0.5, 1.0),
        "w_gate1": gaussian(splits[6], (D, D), D ** -0.5, 0.25),
        "gate1_gain": jnp.clip(jnp.exp(jax.random.uniform(splits[7], (D,), jnp.float32, math.log(0.5), math.log(2.0))), 0.5, 2.0),
        "gate1_shift": gaussian(splits[8], (D,), 0.5, 3.0, (), jnp.float32),
        "ln2_gain": jnp.clip(1.0 + 0.1 * jax.random.normal(splits[9], (D,), jnp.float32), 0.5, 1.5),
        "ln2_bias": gaussian(splits[10], (D,), 0.5, 3.0, (), jnp.float32),
        "w_up": gaussian(splits[11], (D, FF), D ** -0.5, 0.25),
        "b_up": gaussian(splits[12], (FF,), 0.5, 3.0, (), jnp.float32),
        "w_down": gaussian(splits[13], (FF, D), (FF // 2) ** -0.5, 0.1875),
        "b_down": gaussian(splits[14], (D,), 0.5, 3.0, (), jnp.float32),
        "w_gate2": gaussian(splits[15], (D, D), D ** -0.5, 0.25),
        "gate2_gain": jnp.clip(jnp.exp(jax.random.uniform(splits[16], (D,), jnp.float32, math.log(0.5), math.log(2.0))), 0.5, 2.0),
        "gate2_shift": gaussian(splits[17], (D,), 0.5, 3.0, (), jnp.float32),
        "cotangent": gaussian(splits[18], (TOKENS, D), 1.0, 6.0, ((0, 32),)),
    }


@jax.custom_vjp
def low(v):
    return lax.optimization_barrier(v.astype(jnp.bfloat16)).astype(jnp.float32)

@jax.custom_vjp
def low_back(v):
    return v

def low_keep(v):
    return (low(v), None)

def low_pass(kept, grad):
    return (grad,)

def back_keep(v):
    return (v, None)

def back_low(kept, grad):
    return (low(grad),)
low.defvjp(low_keep, low_pass)
low_back.defvjp(back_keep, back_low)
EPS = 1e-05
MASKED = -1e+30

def matmul(left, right):
    return jnp.dot(left, right, precision=lax.Precision.HIGHEST, preferred_element_type=jnp.float32)

def layer_norm(value, gain, shift):
    mean = lax.optimization_barrier(jnp.mean(value, axis=-1, keepdims=True))
    centered = value - mean
    var = lax.optimization_barrier(jnp.mean(centered * centered, axis=-1, keepdims=True))
    return centered * lax.rsqrt(var + EPS) * gain + shift

def batch_gate(logits, gain, shift):
    mean = lax.optimization_barrier(jnp.mean(logits, axis=0, keepdims=True))
    centered = logits - mean
    var = lax.optimization_barrier(jnp.mean(centered * centered, axis=0, keepdims=True))
    return jax.nn.sigmoid(centered * lax.rsqrt(var + EPS) * gain + shift)

def continuation(lengths, span):
    starts = (jnp.cumsum(lengths) - lengths).astype(jnp.int32)
    begins = jnp.arange(lengths.shape[0], dtype=jnp.int32) * span
    hit = (starts[None, :] == begins[:, None]) & (lengths[None, :] > 0)
    return (1 - lax.optimization_barrier(jnp.max(hit.astype(jnp.int32), axis=1))).astype(jnp.int32)

def attention(query, keys, values, flags):
    pad = jnp.zeros((SHORT, HEADS, HD), query.dtype)
    key_ext = jnp.concatenate([pad, keys], axis=0)
    value_ext = jnp.concatenate([pad, values], axis=0)
    scale = HD ** (-0.5)
    rows = lax.broadcasted_iota(jnp.int32, (SHORT, 2 * SHORT), 0)
    cols = lax.broadcasted_iota(jnp.int32, (SHORT, 2 * SHORT), 1)

    def one_block(item):
        index, flag = item
        start = (index * SHORT).astype(jnp.int32)
        q_block = lax.dynamic_slice_in_dim(query, start, SHORT, 0)
        k_block = lax.dynamic_slice_in_dim(key_ext, start, 2 * SHORT, 0)
        v_block = lax.dynamic_slice_in_dim(value_ext, start, 2 * SHORT, 0)
        raw = jnp.einsum('qhd,khd->hqk', q_block, k_block, precision=lax.Precision.HIGHEST) * scale
        scores = low_back(raw)
        allowed = (cols <= rows + SHORT) & ((cols >= SHORT) | (flag > 0))
        scores = jnp.where(allowed[None], scores, MASKED)
        top = lax.optimization_barrier(jnp.max(scores, axis=-1, keepdims=True))
        weights = jnp.exp(scores - top)
        probs = weights / lax.optimization_barrier(jnp.sum(weights, axis=-1, keepdims=True))
        return jnp.einsum('hqk,khd->qhd', low(probs), v_block, precision=lax.Precision.HIGHEST)
    count = query.shape[0] // SHORT
    outs = lax.map(jax.checkpoint(one_block), (jnp.arange(count, dtype=jnp.int32), flags))
    return outs.reshape(query.shape)

def forward(x, ln1_gain, ln1_bias, w_qkv, w_out, w_gate1, gate1_gain, gate1_shift, ln2_gain, ln2_bias, w_up, b_up, w_down, b_down, w_gate2, gate2_gain, gate2_shift, flags):
    total = x.shape[0]
    h1 = low(layer_norm(x, ln1_gain, ln1_bias))
    qkv = low(low_back(matmul(h1, w_qkv)))
    query = qkv[:, :D].reshape(total, HEADS, HD)
    keys = qkv[:, D:2 * D].reshape(total, HEADS, HD)
    values = qkv[:, 2 * D:].reshape(total, HEADS, HD)
    attended = attention(query, keys, values, flags).reshape(total, D)
    attended = low(low_back(attended))
    branch = low_back(matmul(attended, w_out))
    gate_one = batch_gate(low_back(matmul(h1, w_gate1)), gate1_gain, gate1_shift)
    mixed = gate_one * branch + (1.0 - gate_one) * x
    h2 = low(layer_norm(mixed, ln2_gain, ln2_bias))
    pre = low_back(matmul(h2, w_up) + b_up)
    act = low(jax.nn.gelu(pre))
    mlp = low_back(matmul(act, w_down) + b_down)
    gate_two = batch_gate(low_back(matmul(h2, w_gate2)), gate2_gain, gate2_shift)
    return gate_two * mlp + (1.0 - gate_two) * mixed

def reference(tokens, seq_lengths, ln1_gain, ln1_bias, w_qkv, w_out, w_gate1, gate1_gain, gate1_shift, ln2_gain, ln2_bias, w_up, b_up, w_down, b_down, w_gate2, gate2_gain, gate2_shift, cotangent):
    flags = jax.vmap(lambda row: continuation(row, SHORT))(seq_lengths).reshape(-1)
    params = [ln1_gain, ln1_bias, w_qkv, w_out, w_gate1, gate1_gain, gate1_shift, ln2_gain, ln2_bias, w_up, b_up, w_down, b_down, w_gate2, gate2_gain, gate2_shift]
    params = [p.astype(jnp.float32) for p in params]

    def wrapped(*values):
        return forward(*values, flags)
    output, pull = jax.vjp(wrapped, tokens.astype(jnp.float32), *params)
    grads = pull(cotangent.astype(jnp.float32))
    return (output.astype(jnp.bfloat16), grads[0], grads[1], grads[2], grads[3], grads[4], grads[5], grads[6], grads[7], grads[8], grads[9], grads[10], grads[11], grads[12], grads[13], grads[14], grads[15], grads[16])
```

```python
import functools

import jax
import jax.numpy as jnp
from jax import lax
from jax.experimental import pallas as pl
from jax.experimental.pallas import tpu as pltpu
from jax.sharding import PartitionSpec as P

HD = 64
SPAN = 512
HALF = 256
PAIR = 128
EPS = 1e-05
MASKED = -1e30
SCALE = 0.125
AXES = ("seq", "head")
MIB = 1024 * 1024

F32 = jnp.float32
BF16 = jnp.bfloat16


def dot(a, b):
    return jnp.dot(a, b, preferred_element_type=F32)


def dot_nt(a, b):
    return lax.dot_general(a, b, (((1,), (1,)), ((), ())), preferred_element_type=F32)


def dot_tn(a, b):
    return lax.dot_general(a, b, (((0,), (0,)), ((), ())), preferred_element_type=F32)


def struct(shape, dtype):
    return jax.ShapeDtypeStruct(shape, dtype)


def params(mib, dims=1):
    return pltpu.CompilerParams(
        vmem_limit_bytes=mib * MIB, dimension_semantics=("arbitrary",) * dims
    )


def cost(flops, nbytes, trans=0):
    return pl.CostEstimate(flops=int(flops), bytes_accessed=int(nbytes), transcendentals=int(trans))


def rows_of(width, tile=SPAN):
    return pl.BlockSpec((tile, width), lambda i: (i, 0))


def whole(shape):
    return pl.BlockSpec(shape, lambda *_: (0,) * len(shape))


def normed(v):
    centered = v - jnp.mean(v, axis=-1, keepdims=True)
    rstd = lax.rsqrt(jnp.mean(centered * centered, axis=-1, keepdims=True) + EPS)
    return centered * rstd, rstd


def row(ref):
    return ref[...].reshape(1, -1)


def column_sum(v):
    return jnp.sum(v, axis=0, keepdims=True)


def add_stats(acc, z, i):
    n = z.shape[0]
    mean = column_sum(z) * (1.0 / n)
    c = z - mean
    dev = column_sum(c * c)

    @pl.when(i == 0)
    def _():
        acc[0:1, :] = mean
        acc[1:2, :] = dev

    @pl.when(i > 0)
    def _():
        before = i.astype(F32)
        gap = mean - acc[0:1, :]
        acc[0:1, :] += gap / (before + 1.0)
        acc[1:2, :] += dev + gap * gap * (n * before / (before + 1.0))


def add_sums(acc, sums, i):
    for j, s in enumerate(sums):

        @pl.when(i == 0)
        def _(j=j, s=s):
            acc[j : j + 1, :] = s

        @pl.when(i > 0)
        def _(j=j, s=s):
            acc[j : j + 1, :] += s


def spread(acc, out):
    out[...] = jnp.broadcast_to(acc[...][None], out.shape)


def merge_stats(parts, rows):
    n = parts.shape[0]
    means = parts[:, 0, :]
    mean = jnp.mean(means, axis=0, keepdims=True)
    gaps = means - mean
    dev = jnp.sum(parts[:, 1, :], axis=0, keepdims=True) + rows * jnp.sum(
        gaps * gaps, axis=0, keepdims=True
    )
    return mean, lax.rsqrt(dev * (1.0 / (rows * n)) + EPS)


def exchange(spread_rows):
    return lax.all_to_all(spread_rows, AXES, 0, 0, tiled=True)


def first_kernel(x, gain, bias, w_qkv, w_gate, h1, qkv, z1, stats, acc):
    i = pl.program_id(0)
    n, _ = normed(x[...].astype(F32))
    h = (n * row(gain) + row(bias)).astype(BF16)
    h1[...] = h
    qkv[...] = dot(h, w_qkv[...]).astype(BF16)
    z = dot(h, w_gate[...])
    z1[...] = z
    add_stats(acc, z, i)

    @pl.when(i == pl.num_programs(0) - 1)
    def _():
        spread(acc, stats)


def halo_kernel(x, gain, bias, w_qkv, kv):
    n, _ = normed(x[...].astype(F32))
    h = (n * row(gain) + row(bias)).astype(BF16)
    width = x.shape[1]
    kv[...] = dot(h, w_qkv[:, width:]).astype(BF16)


def diagonal():
    rows = lax.broadcasted_iota(jnp.int32, (HALF, HALF), 0)
    cols = lax.broadcasted_iota(jnp.int32, (HALF, HALF), 1)
    return rows, cols


def attend_kernel(flags, q, k, v, kp, vp, kh, vh, out, lse):
    b = pl.program_id(1)
    low = lax.broadcasted_iota(jnp.int32, (1, PAIR), 1) < HD

    def compute(wide):
        rows, cols = diagonal()
        allowed = cols <= rows
        if wide:
            first = b == 0
            k_prev = jnp.where(first, kh[...], kp[...])
            v_prev = jnp.where(first, vh[...], vp[...])
        for half in range(2):
            at = slice(half * HALF, (half + 1) * HALF)
            q_half = q[at, :] * jnp.asarray(SCALE, BF16)
            outs, tops = [], []
            for s in range(2):
                q_s = jnp.where(low if s == 0 else ~low, q_half, jnp.zeros_like(q_half))
                pieces = [(jnp.where(allowed, dot_nt(q_s, k[at, :]), MASKED), v[at, :])]
                if half:
                    pieces.append((dot_nt(q_s, k[:HALF, :]), v[:HALF, :]))
                if wide:
                    pieces.append((dot_nt(q_s, k_prev), v_prev))
                top = functools.reduce(
                    jnp.maximum, [jnp.max(p, axis=-1, keepdims=True) for p, _ in pieces]
                )
                total, acc = 0.0, 0.0
                for p, vals in pieces:
                    e = jnp.exp(p - top)
                    total = total + jnp.sum(e, axis=-1, keepdims=True)
                    acc = acc + dot(e.astype(BF16), vals)
                outs.append(acc / total)
                tops.append(top + jnp.log(total))
            out[at, :] = jnp.where(low, outs[0], outs[1]).astype(BF16)
            turned = jnp.where(low, tops[0], tops[1]).T
            lse[0, 0:1, at] = turned[0:1, :]
            lse[0, 1:2, at] = turned[HD : HD + 1, :]

    wide = flags[b] > 0
    pl.when(wide)(functools.partial(compute, True))
    pl.when(jnp.logical_not(wide))(functools.partial(compute, False))


def mix_kernel(
    rows, att, x, z1, parts, gain, shift, ln_gain, ln_bias, w_out, w_gate, y1, h2, z2, stats, acc, st
):
    i = pl.program_id(0)

    @pl.when(i == 0)
    def _():
        mean, rstd = merge_stats(parts, rows)
        st[0:1, :] = mean
        st[1:2, :] = rstd

    branch = dot(att[...], w_out[...])
    nhat = (z1[...] - st[0:1, :]) * st[1:2, :]
    t = jax.nn.sigmoid(nhat * row(gain) + row(shift))
    y = t * branch + (1.0 - t) * x[...].astype(F32)
    y1[...] = y
    n, _ = normed(y)
    h = (n * row(ln_gain) + row(ln_bias)).astype(BF16)
    h2[...] = h
    z = dot(h, w_gate[...])
    z2[...] = z
    add_stats(acc, z, i)

    @pl.when(i == pl.num_programs(0) - 1)
    def _():
        spread(acc, stats)


GELU_C = 0.7978845608028654
GELU_A = 0.044715


def mlp_kernel(h2, w_up, b_up, w_down, b_down, act, slope, mlp):
    h = h2[...]
    units = w_up.shape[1]
    total = row(b_down)
    step = 512
    bias = row(b_up)
    for j in range(units // step):
        at = slice(j * step, (j + 1) * step)
        pre = dot(h, w_up[:, at]) + bias[:, at]
        sq = pre * pre
        th = jnp.tanh(pre * (GELU_C + (GELU_C * GELU_A) * sq))
        cdf = 0.5 + 0.5 * th
        a = (pre * cdf).astype(BF16)
        g = cdf + pre * (0.5 - 0.5 * th * th) * (GELU_C + (3.0 * GELU_C * GELU_A) * sq)
        act[:, at] = a
        slope[:, at] = g.astype(BF16)
        total = total + dot(a, w_down[at, :])
    mlp[...] = total


def gate2_kernel(rows, mlp, y1, z2, c, parts, gain, shift, out, dmlp, sums, acc, st):
    i = pl.program_id(0)

    @pl.when(i == 0)
    def _():
        mean, rstd = merge_stats(parts, rows)
        st[0:1, :] = mean
        st[1:2, :] = rstd

    nhat = (z2[...] - st[0:1, :]) * st[1:2, :]
    t = jax.nn.sigmoid(nhat * row(gain) + row(shift))
    m, y = mlp[...], y1[...]
    out[...] = (t * m + (1.0 - t) * y).astype(BF16)
    g = c[...].astype(F32)
    dmlp[...] = (g * t).astype(BF16)
    du = g * (m - y) * t * (1.0 - t)
    add_sums(acc, [column_sum(du), column_sum(du * nhat)], i)

    @pl.when(i == pl.num_programs(0) - 1)
    def _():
        spread(acc, sums)


def mlp_back_kernel(dmlp, act, slope, h2, w_up, w_down, dh2, g_up, g_down, g_b, acc_up, acc_down):
    i = pl.program_id(0)

    @pl.when(i == 0)
    def _():
        acc_up[...] = jnp.zeros_like(acc_up)
        acc_down[...] = jnp.zeros_like(acc_down)
        g_b[...] = jnp.zeros_like(g_b)

    d, h = dmlp[...], h2[...]
    units = w_up.shape[1]
    step = 512
    total = 0.0
    width = d.shape[1]
    for j in range(units // step):
        at = slice(j * step, (j + 1) * step)
        dp = (dot_nt(d, w_down[at, :]) * slope[:, at].astype(F32)).astype(BF16)
        g_b[0:1, at] += column_sum(dp.astype(F32))
        total = total + dot_nt(dp, w_up[:, at])
        acc_up[:, at] += dot_tn(h, dp)
        acc_down[:, at] += dot_tn(d, act[:, at])
    dh2[...] = total
    g_b[1:2, 0:width] += column_sum(d.astype(F32))

    @pl.when(i == pl.num_programs(0) - 1)
    def _():
        g_up[...] = acc_up[...].astype(BF16)
        for j in range(units // step):
            at = slice(j * step, (j + 1) * step)
            g_down[at, :] = acc_down[:, at].T.astype(BF16)


def middle_kernel(
    rows,
    c,
    mlp,
    y1,
    z2,
    dh2p,
    att,
    x,
    z1,
    h2,
    parts2,
    sums2,
    parts1,
    gain2,
    shift2,
    gain1,
    shift1,
    ln_gain,
    w_gate2,
    w_out,
    gx,
    du1,
    datt,
    delta,
    g_w,
    sums,
    g_gate2,
    acc,
    st,
    acc_gate,
    acc_out,
):
    i = pl.program_id(0)
    count = 1.0 / (rows * parts2.shape[0])
    width = y1.shape[1]

    @pl.when(i == 0)
    def _():
        mean, rstd = merge_stats(parts2, rows)
        st[0:1, :] = mean
        st[1:2, :] = rstd
        mean, rstd = merge_stats(parts1, rows)
        st[2:3, :] = mean
        st[3:4, :] = rstd
        st[4:5, :] = jnp.sum(sums2[:, 0, :], axis=0, keepdims=True)
        st[5:6, :] = jnp.sum(sums2[:, 1, :], axis=0, keepdims=True)
        g_gate2[...] = st[4:6, :]
        acc_gate[...] = jnp.zeros_like(acc_gate)
        acc_out[...] = jnp.zeros_like(acc_out)

    g = c[...].astype(F32)
    y = y1[...]
    nhat2 = (z2[...] - st[0:1, :]) * st[1:2, :]
    t2 = jax.nn.sigmoid(nhat2 * row(gain2) + row(shift2))
    du2 = g * (mlp[...] - y) * t2 * (1.0 - t2)
    dz2 = (
        (row(gain2) * st[1:2, :]) * (du2 - st[4:5, :] * count - nhat2 * (st[5:6, :] * count))
    ).astype(BF16)
    acc_gate[...] += dot_tn(h2[...], dz2)
    dh2 = dh2p[...] + dot_nt(dz2, w_gate2[...])
    n, r = normed(y)
    e = dh2 * row(ln_gain)
    dy = g * (1.0 - t2) + r * (
        e - jnp.mean(e, axis=-1, keepdims=True) - n * jnp.mean(e * n, axis=-1, keepdims=True)
    )
    a = att[...]
    branch = dot(a, w_out[...])
    nhat1 = (z1[...] - st[2:3, :]) * st[3:4, :]
    t1 = jax.nn.sigmoid(nhat1 * row(gain1) + row(shift1))
    dbranch = (dy * t1).astype(BF16)
    gx[...] = dy * (1.0 - t1)
    du = dy * (branch - x[...].astype(F32)) * t1 * (1.0 - t1)
    du1[...] = du
    acc_out[...] += dot_tn(a, dbranch)
    da = dot_nt(dbranch, w_out[...]).astype(BF16)
    datt[...] = da
    prod = da.astype(F32) * a.astype(F32)
    hi = prod.astype(BF16)
    lo = (prod - hi.astype(F32)).astype(BF16)
    heads = width // HD
    pick = (
        lax.broadcasted_iota(jnp.int32, (heads, width), 1) // HD
        == lax.broadcasted_iota(jnp.int32, (heads, width), 0)
    ).astype(BF16)
    dl = dot_nt(pick, hi) + dot_nt(pick, lo)
    for p in range(heads // 2):
        delta[p] = dl[2 * p : 2 * p + 2, :]
    add_sums(
        acc, [column_sum(du), column_sum(du * nhat1), column_sum(dh2 * n), column_sum(dh2)], i
    )

    @pl.when(i == pl.num_programs(0) - 1)
    def _():
        spread(acc, sums)
        g_w[0:width, :] = acc_gate[...].astype(BF16)
        g_w[width:, :] = acc_out[...].astype(BF16)


def attend_back_unit(q_s, do_s, k_c, v_c, kt_s, lse, delta, mask):
    p = jnp.exp(dot_nt(k_c, q_s) - lse)
    if mask is not None:
        p = jnp.where(mask, p, 0.0)
    ds = (p * (dot_nt(v_c, do_s) - delta)).astype(BF16)
    return dot(ds, q_s), dot(p.astype(BF16), do_s), dot(kt_s, ds)


def head_inputs(q, do, s, low):
    pick = low if s == 0 else ~low
    q_s = jnp.where(pick, q, jnp.zeros_like(q)) * jnp.asarray(SCALE, BF16)
    do_s = jnp.where(pick, do, jnp.zeros_like(do))
    return q_s, do_s


def own_terms(q, do, k, v, lse, delta, low, dq_t, dk, dv):
    kt = k.T * jnp.asarray(SCALE, BF16)
    rows, cols = diagonal()
    mask = rows <= cols
    wide_mask = jnp.concatenate([mask, jnp.ones((HALF, HALF), jnp.bool_)], axis=1)
    k0, k1 = [0.0, 0.0], [0.0, 0.0]
    for s in range(2):
        q_s, do_s = head_inputs(q, do, s, low)
        ls, de = lse[s : s + 1, :], delta[s : s + 1, :]
        kt_s = kt[s * HD : (s + 1) * HD, :]
        a, b, c = attend_back_unit(
            q_s, do_s, k[:HALF], v[:HALF], kt_s[:, :HALF], ls, de, wide_mask
        )
        k0[0] = k0[0] + a
        k0[1] = k0[1] + b
        dq_t[s * HD : (s + 1) * HD, :] = c
        a, b, c = attend_back_unit(
            q_s[HALF:],
            do_s[HALF:],
            k[HALF:],
            v[HALF:],
            kt_s[:, HALF:],
            ls[:, HALF:],
            de[:, HALF:],
            mask,
        )
        k1[0] = k1[0] + a
        k1[1] = k1[1] + b
        dq_t[s * HD : (s + 1) * HD, HALF:] += c
    dk[:HALF, :] = k0[0]
    dk[HALF:, :] = k1[0]
    dv[:HALF, :] = k0[1]
    dv[HALF:, :] = k1[1]


def before_terms(q, do, k, v, lse, delta, low, dq_t):
    kt = k.T * jnp.asarray(SCALE, BF16)
    dk, dv = 0.0, 0.0
    for s in range(2):
        q_s, do_s = head_inputs(q, do, s, low)
        a, b, c = attend_back_unit(
            q_s,
            do_s,
            k,
            v,
            kt[s * HD : (s + 1) * HD, :],
            lse[s : s + 1, :],
            delta[s : s + 1, :],
            None,
        )
        dk = dk + a
        dv = dv + b
        dq_t[s * HD : (s + 1) * HD, :] += c
    return dk, dv


def back_first_kernel(flags, q, do, k, v, kh, vh, lse, delta, dq, dk, dv, terms, dq_t):
    low = lax.broadcasted_iota(jnp.int32, (1, PAIR), 1) < HD
    ls, de = lse[0], delta[0]
    own_terms(q[...], do[...], k[...], v[...], ls, de, low, dq_t, dk, dv)
    wide = flags[0] > 0

    @pl.when(wide)
    def _():
        a, b = before_terms(q[...], do[...], kh[...], vh[...], ls, de, low, dq_t)
        terms[0] = a.astype(BF16)
        terms[1] = b.astype(BF16)

    @pl.when(jnp.logical_not(wide))
    def _():
        terms[...] = jnp.zeros_like(terms)

    dq[...] = dq_t[...].T.astype(BF16)


def back_rest_kernel(
    flags, q, do, k, v, kp, vp, lse, delta, dq0, dk0, dv0, dq, dk, dv, last, dq_t, carry, own
):
    low = lax.broadcasted_iota(jnp.int32, (1, PAIR), 1) < HD
    j = pl.program_id(1)
    blocks = pl.num_programs(1)
    b = blocks - 1 - j

    @pl.when(b > 0)
    def _():
        ls, de = lse[0], delta[0]
        own_terms(q[...], do[...], k[...], v[...], ls, de, low, dq_t, own.at[0], own.at[1])

        @pl.when(j == 0)
        def _():
            last[...] = own[...]

        @pl.when(j > 0)
        def _():
            dk[...] = (own[0] + carry[0]).astype(BF16)
            dv[...] = (own[1] + carry[1]).astype(BF16)

        wide = flags[b] > 0

        @pl.when(wide)
        def _():
            a, bb = before_terms(q[...], do[...], kp[...], vp[...], ls, de, low, dq_t)
            carry[0] = a
            carry[1] = bb

        @pl.when(jnp.logical_not(wide))
        def _():
            carry[...] = jnp.zeros_like(carry)

        dq[...] = dq_t[...].T.astype(BF16)

    @pl.when(b == 0)
    def _():
        dq[...] = dq0[...]
        dk[...] = (dk0[...] + carry[0]).astype(BF16)
        dv[...] = (dv0[...] + carry[1]).astype(BF16)


def last_kernel(
    rows,
    h1,
    dq,
    dk,
    dv,
    last,
    arrived,
    du1,
    z1,
    x,
    gx,
    parts1,
    sums1,
    gain1,
    ln_gain,
    w_qkv,
    w_gate1,
    grad_x,
    g_w,
    sums,
    g_gate1,
    acc,
    st,
    dqkv,
):
    i = pl.program_id(0)
    final = i == pl.num_programs(0) - 1
    count = 1.0 / (rows * parts1.shape[0])
    width = x.shape[1]

    @pl.when(i == 0)
    def _():
        mean, rstd = merge_stats(parts1, rows)
        st[2:3, :] = mean
        st[3:4, :] = rstd
        st[4:5, :] = jnp.sum(sums1[:, 0, :], axis=0, keepdims=True)
        st[5:6, :] = jnp.sum(sums1[:, 1, :], axis=0, keepdims=True)
        g_gate1[0:2, :] = st[4:6, :]
        g_gate1[2:3, :] = jnp.sum(sums1[:, 2, :], axis=0, keepdims=True)
        g_gate1[3:4, :] = jnp.sum(sums1[:, 3, :], axis=0, keepdims=True)
        acc[...] = jnp.zeros_like(acc)

    nhat = (z1[...] - st[2:3, :]) * st[3:4, :]
    dz = (
        (row(gain1) * st[3:4, :]) * (du1[...] - st[4:5, :] * count - nhat * (st[5:6, :] * count))
    ).astype(BF16)
    dqkv[:, :width] = dq[...]

    @pl.when(jnp.logical_not(final))
    def _():
        dqkv[:, width : 2 * width] = dk[...]
        dqkv[:, 2 * width :] = dv[...]

    @pl.when(final)
    def _():
        dqkv[:, width : 2 * width] = (last[0] + arrived[0].astype(F32)).astype(BF16)
        dqkv[:, 2 * width :] = (last[1] + arrived[1].astype(F32)).astype(BF16)

    h = h1[...]
    d = dqkv[...]
    acc[:, : 3 * width] += dot_tn(h, d)
    acc[:, 3 * width :] += dot_tn(h, dz)
    dh = dot_nt(d, w_qkv[...]) + dot_nt(dz, w_gate1[...])
    n, r = normed(x[...].astype(F32))
    e = dh * row(ln_gain)
    grad_x[...] = gx[...] + r * (
        e - jnp.mean(e, axis=-1, keepdims=True) - n * jnp.mean(e * n, axis=-1, keepdims=True)
    )
    add_sums(sums, [column_sum(dh * n), column_sum(dh)], i)

    @pl.when(final)
    def _():
        g_w[...] = acc[...].astype(BF16)


def stage_list():
    out = []
    for axis in AXES:
        bit = 1
        while bit < lax.axis_size(axis):
            out.append((axis, bit))
            bit *= 2
    return out


def swap(x, axis, bit):
    n = lax.axis_size(axis)
    return lax.ppermute(x, axis, [(i, i ^ bit) for i in range(n)])


def upper(axis, bit):
    return (lax.axis_index(axis) & bit) // bit


def sum_everywhere(g):
    stages = stage_list()
    for axis, bit in stages:
        half = g.shape[0] // 2
        mine = upper(axis, bit)
        send = lax.dynamic_slice_in_dim(g, (1 - mine) * half, half, 0)
        keep = lax.dynamic_slice_in_dim(g, mine * half, half, 0)
        got = swap(send, axis, bit)
        g = (keep.astype(F32) + got.astype(F32)).astype(g.dtype)
    for axis, bit in reversed(stages):
        got = swap(g, axis, bit)
        up = upper(axis, bit) > 0
        g = jnp.concatenate([jnp.where(up, got, g), jnp.where(up, g, got)], axis=0)
    return g


def sum_small(v):
    for axis, bit in stage_list():
        v = v + swap(v, axis, bit)
    return v


def continuation(lengths, span):
    place = jnp.arange(lengths.shape[0], dtype=jnp.int32)
    starts = jnp.sum(jnp.where(place[None, :] < place[:, None], lengths[None, :], 0), axis=1)
    begins = place * span
    hit = (starts[None, :] == begins[:, None]) & (lengths[None, :] > 0)
    return 1 - jnp.max(hit.astype(jnp.int32), axis=1)


def body(
    tokens,
    seq_lengths,
    ln1_gain,
    ln1_bias,
    w_qkv,
    w_out,
    w_gate1,
    gate1_gain,
    gate1_shift,
    ln2_gain,
    ln2_bias,
    w_up,
    b_up,
    w_down,
    b_down,
    w_gate2,
    gate2_gain,
    gate2_shift,
    cotangent,
):
    rows, width = tokens.shape
    units = w_up.shape[1]
    ndev = lax.axis_size("seq") * lax.axis_size("head")
    blocks = rows // SPAN
    pairs = width // PAIR
    heads = width // HD
    count = lax.axis_size("head")
    mac = rows * width * width

    tail = tokens[rows - SPAN :]
    before = lax.ppermute(tail, "head", [(i, i + 1) for i in range(count - 1)])
    flags = lax.dynamic_slice_in_dim(
        continuation(seq_lengths[0], SPAN), lax.axis_index("head") * blocks, blocks, 0
    )

    vec = whole((width,))
    stats_shape = (ndev, 2, width)
    h1, qkv, z1, stats1 = pl.pallas_call(
        first_kernel,
        grid=(blocks,),
        in_specs=[rows_of(width), vec, vec, whole(w_qkv.shape), whole(w_gate1.shape)],
        out_specs=[rows_of(width), rows_of(3 * width), rows_of(width), whole(stats_shape)],
        out_shape=[
            struct((rows, width), BF16),
            struct((rows, 3 * width), BF16),
            struct((rows, width), F32),
            struct(stats_shape, F32),
        ],
        scratch_shapes=[pltpu.VMEM((2, width), F32)],
        compiler_params=params(40),
        cost_estimate=cost(8 * mac, rows * width * 14, rows),
        name="first",
    )(tokens, ln1_gain, ln1_bias, w_qkv, w_gate1)
    parts1 = exchange(stats1)

    kv_halo = pl.pallas_call(
        halo_kernel,
        out_shape=struct((SPAN, 2 * width), BF16),
        compiler_params=pltpu.CompilerParams(vmem_limit_bytes=20 * MIB),
        cost_estimate=cost(4 * SPAN * width * width, 4 * MIB, SPAN),
        name="halo",
    )(before, ln1_gain, ln1_bias, w_qkv)

    def tile(f):
        return pl.BlockSpec((SPAN, PAIR), f)

    att, lse = pl.pallas_call(
        attend_kernel,
        grid_spec=pltpu.PrefetchScalarGridSpec(
            num_scalar_prefetch=1,
            grid=(pairs, blocks),
            in_specs=[
                tile(lambda p, b, f: (b, p)),
                tile(lambda p, b, f: (b, pairs + p)),
                tile(lambda p, b, f: (b, 2 * pairs + p)),
                tile(lambda p, b, f: (jnp.maximum(b - 1, 0), pairs + p)),
                tile(lambda p, b, f: (jnp.maximum(b - 1, 0), 2 * pairs + p)),
                tile(lambda p, b, f: (0, p)),
                tile(lambda p, b, f: (0, pairs + p)),
            ],
            out_specs=[
                tile(lambda p, b, f: (b, p)),
                pl.BlockSpec((1, 2, SPAN), lambda p, b, f: (p, 0, b)),
            ],
        ),
        out_shape=[struct((rows, width), BF16), struct((pairs, 2, rows), F32)],
        compiler_params=params(32, 2),
        cost_estimate=cost(10 * heads * SPAN * SPAN * PAIR * 4, 12 * MIB, heads * SPAN * SPAN * 5),
        name="attend",
    )(flags, qkv, qkv, qkv, qkv, qkv, kv_halo, kv_halo)

    y1, h2, z2, stats2 = pl.pallas_call(
        functools.partial(mix_kernel, rows),
        grid=(blocks,),
        in_specs=[rows_of(width), rows_of(width), rows_of(width), whole(stats_shape)]
        + [vec] * 4
        + [whole(w_out.shape), whole(w_gate2.shape)],
        out_specs=[rows_of(width), rows_of(width), rows_of(width), whole(stats_shape)],
        out_shape=[
            struct((rows, width), F32),
            struct((rows, width), BF16),
            struct((rows, width), F32),
            struct(stats_shape, F32),
        ],
        scratch_shapes=[pltpu.VMEM((2, width), F32), pltpu.VMEM((8, width), F32)],
        compiler_params=params(40),
        cost_estimate=cost(4 * mac, rows * width * 18, rows * width),
        name="mix",
    )(att, tokens, z1, parts1, gate1_gain, gate1_shift, ln2_gain, ln2_bias, w_out, w_gate2)
    parts2 = exchange(stats2)

    act, slope, mlp = pl.pallas_call(
        mlp_kernel,
        grid=(blocks,),
        in_specs=[
            rows_of(width),
            whole(w_up.shape),
            whole((units,)),
            whole(w_down.shape),
            vec,
        ],
        out_specs=[rows_of(units), rows_of(units), rows_of(width)],
        out_shape=[
            struct((rows, units), BF16),
            struct((rows, units), BF16),
            struct((rows, width), F32),
        ],
        compiler_params=params(48),
        cost_estimate=cost(4 * rows * width * units, rows * units * 4, rows * units),
        name="mlp",
    )(h2, w_up, b_up, w_down, b_down)

    output, dmlp, sums2 = pl.pallas_call(
        functools.partial(gate2_kernel, rows),
        grid=(blocks,),
        in_specs=[rows_of(width)] * 4 + [whole(stats_shape), vec, vec],
        out_specs=[rows_of(width), rows_of(width), whole(stats_shape)],
        out_shape=[
            struct((rows, width), BF16),
            struct((rows, width), BF16),
            struct(stats_shape, F32),
        ],
        scratch_shapes=[pltpu.VMEM((2, width), F32), pltpu.VMEM((8, width), F32)],
        compiler_params=params(40),
        cost_estimate=cost(rows * width * 20, rows * width * 18, rows * width),
        name="gate2",
    )(mlp, y1, z2, cotangent, parts2, gate2_gain, gate2_shift)
    parts_du2 = exchange(sums2)

    dh2p, g_up, g_down, g_b = pl.pallas_call(
        mlp_back_kernel,
        grid=(blocks,),
        in_specs=[
            rows_of(width),
            rows_of(units),
            rows_of(units),
            rows_of(width),
            whole(w_up.shape),
            whole(w_down.shape),
        ],
        out_specs=[
            rows_of(width),
            whole(w_up.shape),
            whole(w_down.shape),
            whole((2, units)),
        ],
        out_shape=[
            struct((rows, width), F32),
            struct(w_up.shape, BF16),
            struct(w_down.shape, BF16),
            struct((2, units), F32),
        ],
        scratch_shapes=[pltpu.VMEM((width, units), F32), pltpu.VMEM((width, units), F32)],
        compiler_params=params(56),
        cost_estimate=cost(8 * rows * width * units, rows * units * 5),
        name="mlp_back",
    )(dmlp, act, slope, h2, w_up, w_down)

    sums_shape = (ndev, 4, width)
    rows_pair = pl.BlockSpec((pairs, 2, SPAN), lambda i: (0, 0, i))
    gx, du1, datt, delta, g_mid, sums1, g_gate2 = pl.pallas_call(
        functools.partial(middle_kernel, rows),
        grid=(blocks,),
        in_specs=[rows_of(width)] * 9
        + [whole(stats_shape)] * 3
        + [vec] * 5
        + [whole(w_gate2.shape), whole(w_out.shape)],
        out_specs=[
            rows_of(width),
            rows_of(width),
            rows_of(width),
            rows_pair,
            whole((2 * width, width)),
            whole(sums_shape),
            whole((2, width)),
        ],
        out_shape=[
            struct((rows, width), F32),
            struct((rows, width), F32),
            struct((rows, width), BF16),
            struct((pairs, 2, rows), F32),
            struct((2 * width, width), BF16),
            struct(sums_shape, F32),
            struct((2, width), F32),
        ],
        scratch_shapes=[
            pltpu.VMEM((4, width), F32),
            pltpu.VMEM((8, width), F32),
            pltpu.VMEM((width, width), F32),
            pltpu.VMEM((width, width), F32),
        ],
        compiler_params=params(56),
        cost_estimate=cost(10 * mac, rows * width * 38, rows * width * 2),
        name="middle",
    )(
        cotangent,
        mlp,
        y1,
        z2,
        dh2p,
        att,
        tokens,
        z1,
        h2,
        parts2,
        parts_du2,
        parts1,
        gate2_gain,
        gate2_shift,
        gate1_gain,
        gate1_shift,
        ln2_gain,
        w_gate2,
        w_out,
    )
    parts_du1 = exchange(sums1)

    pair_rows = (1, 2, SPAN)
    dq0, dk0, dv0, terms = pl.pallas_call(
        back_first_kernel,
        grid_spec=pltpu.PrefetchScalarGridSpec(
            num_scalar_prefetch=1,
            grid=(pairs,),
            in_specs=[
                tile(lambda p, f: (0, p)),
                tile(lambda p, f: (0, p)),
                tile(lambda p, f: (0, pairs + p)),
                tile(lambda p, f: (0, 2 * pairs + p)),
                tile(lambda p, f: (0, p)),
                tile(lambda p, f: (0, pairs + p)),
                pl.BlockSpec(pair_rows, lambda p, f: (p, 0, 0)),
                pl.BlockSpec(pair_rows, lambda p, f: (p, 0, 0)),
            ],
            out_specs=[
                tile(lambda p, f: (0, p)),
                tile(lambda p, f: (0, p)),
                tile(lambda p, f: (0, p)),
                pl.BlockSpec((2, SPAN, PAIR), lambda p, f: (0, 0, p)),
            ],
            scratch_shapes=[pltpu.VMEM((PAIR, SPAN), F32)],
        ),
        out_shape=[
            struct((SPAN, width), BF16),
            struct((SPAN, width), F32),
            struct((SPAN, width), F32),
            struct((2, SPAN, width), BF16),
        ],
        compiler_params=params(32, 1),
        cost_estimate=cost(
            10 * heads * SPAN * SPAN * PAIR * 2, 8 * MIB, heads * SPAN * SPAN * 2
        ),
        name="attend_back_first",
    )(flags, qkv, datt, qkv, qkv, kv_halo, kv_halo, lse, delta)
    arrived = lax.ppermute(terms, "head", [(i + 1, i) for i in range(count - 1)])

    def at_block(column):
        return tile(lambda p, j, f: (jnp.maximum(blocks - 1 - j, 1), column * pairs + p))

    def at_prev(column):
        return tile(lambda p, j, f: (jnp.maximum(blocks - 2 - j, 0), column * pairs + p))

    def at_first():
        return tile(lambda p, j, f: (0, p))

    def out_block():
        return tile(lambda p, j, f: (blocks - 1 - j, p))

    row_block = pl.BlockSpec(pair_rows, lambda p, j, f: (p, 0, jnp.maximum(blocks - 1 - j, 1)))
    dq, dk, dv, last = pl.pallas_call(
        back_rest_kernel,
        grid_spec=pltpu.PrefetchScalarGridSpec(
            num_scalar_prefetch=1,
            grid=(pairs, blocks),
            in_specs=[
                at_block(0),
                at_block(0),
                at_block(1),
                at_block(2),
                at_prev(1),
                at_prev(2),
                row_block,
                row_block,
                at_first(),
                at_first(),
                at_first(),
            ],
            out_specs=[
                out_block(),
                out_block(),
                out_block(),
                pl.BlockSpec((2, SPAN, PAIR), lambda p, j, f: (0, 0, p)),
            ],
            scratch_shapes=[
                pltpu.VMEM((PAIR, SPAN), F32),
                pltpu.VMEM((2, SPAN, PAIR), F32),
                pltpu.VMEM((2, SPAN, PAIR), F32),
            ],
        ),
        out_shape=[struct((rows, width), BF16)] * 3 + [struct((2, SPAN, width), F32)],
        compiler_params=params(32, 2),
        cost_estimate=cost(
            10 * heads * SPAN * SPAN * PAIR * 6, 20 * MIB, heads * SPAN * SPAN * 4
        ),
        name="attend_back_rest",
    )(flags, qkv, datt, qkv, qkv, qkv, qkv, lse, delta, dq0, dk0, dv0)

    grad_x, g_in, ln1_sums, g_gate1 = pl.pallas_call(
        functools.partial(last_kernel, rows),
        grid=(blocks,),
        in_specs=[rows_of(width)] * 4
        + [whole((2, SPAN, width))] * 2
        + [rows_of(width)] * 4
        + [whole(stats_shape), whole(sums_shape), vec, vec]
        + [whole(w_qkv.shape), whole(w_gate1.shape)],
        out_specs=[
            rows_of(width),
            whole((width, 4 * width)),
            whole((2, width)),
            whole((4, width)),
        ],
        out_shape=[
            struct((rows, width), F32),
            struct((width, 4 * width), BF16),
            struct((2, width), F32),
            struct((4, width), F32),
        ],
        scratch_shapes=[
            pltpu.VMEM((width, 4 * width), F32),
            pltpu.VMEM((8, width), F32),
            pltpu.VMEM((SPAN, 3 * width), BF16),
        ],
        compiler_params=params(56),
        cost_estimate=cost(16 * mac, rows * width * 26),
        name="last",
    )(
        h1,
        dq,
        dk,
        dv,
        last,
        arrived,
        du1,
        z1,
        tokens,
        gx,
        parts1,
        parts_du1,
        gate1_gain,
        ln1_gain,
        w_qkv,
        w_gate1,
    )

    g_down = sum_everywhere(g_down).astype(F32)
    g_up = sum_everywhere(g_up).astype(F32)
    g_mid = sum_everywhere(g_mid).astype(F32)
    g_in = sum_everywhere(g_in).astype(F32)
    g_b = sum_small(g_b)
    ln1_sums = sum_small(ln1_sums)
    return (
        output,
        grad_x,
        ln1_sums[0],
        ln1_sums[1],
        g_in[:, : 3 * width],
        g_mid[width:],
        g_in[:, 3 * width :],
        g_gate1[1],
        g_gate1[0],
        g_gate1[2],
        g_gate1[3],
        g_up,
        g_b[0],
        g_down,
        g_b[1, :width],
        g_mid[:width],
        g_gate2[1],
        g_gate2[0],
    )


def solution(mesh):
    split = P(AXES, None)
    return jax.shard_map(
        body,
        mesh=mesh,
        in_specs=(split, P("seq", None)) + (P(),) * 16 + (split,),
        out_specs=(split, split) + (P(),) * 16,
        check_vma=False,
    )
```

```python
import functools

import jax
import jax.numpy as jnp
from jax import lax
from jax.experimental import pallas as pl
from jax.experimental.pallas import tpu as pltpu
from jax.sharding import PartitionSpec as P

HD = 64
SPAN = 512
HALF = 256
PAIR = 128
PAD = 128
LATE_WEIGHT = 0.02
EPS = 1e-05
MASKED = -1e30
SCALE = 0.125
AXES = ("seq", "head")
MIB = 1024 * 1024
VMEM_MIB = 60

F32 = jnp.float32
BF16 = jnp.bfloat16


def dot(a, b):
    return jnp.dot(a, b, preferred_element_type=F32)


def dot_nt(a, b):
    return lax.dot_general(a, b, (((1,), (1,)), ((), ())), preferred_element_type=F32)


def dot_tn(a, b):
    return lax.dot_general(a, b, (((0,), (0,)), ((), ())), preferred_element_type=F32)


def struct(shape, dtype):
    return jax.ShapeDtypeStruct(shape, dtype)


def params(mib):
    return pltpu.CompilerParams(vmem_limit_bytes=mib * MIB, dimension_semantics=("arbitrary",))


def cost(flops, nbytes, trans=0):
    return pl.CostEstimate(flops=int(flops), bytes_accessed=int(nbytes), transcendentals=int(trans))


def rows_of(width, tile=SPAN):
    return pl.BlockSpec((tile, width), lambda i: (i, 0))


def whole(shape):
    return pl.BlockSpec(shape, lambda *_: (0,) * len(shape))


def normed(v):
    centered = v - jnp.mean(v, axis=-1, keepdims=True)
    rstd = lax.rsqrt(jnp.mean(centered * centered, axis=-1, keepdims=True) + EPS)
    return centered * rstd, rstd


def row(ref):
    return ref[...].reshape(1, -1)


def column_sum(v):
    return jnp.sum(v, axis=0, keepdims=True)


def add_stats(acc, z, i):
    n = z.shape[0]
    mean = column_sum(z) * (1.0 / n)
    c = z - mean
    dev = column_sum(c * c)

    @pl.when(i == 0)
    def _():
        acc[0:1, :] = mean
        acc[1:2, :] = dev

    @pl.when(i > 0)
    def _():
        before = i.astype(F32)
        gap = mean - acc[0:1, :]
        acc[0:1, :] += gap / (before + 1.0)
        acc[1:2, :] += dev + gap * gap * (n * before / (before + 1.0))


def add_sums(acc, sums, i):
    for j, s in enumerate(sums):

        @pl.when(i == 0)
        def _(j=j, s=s):
            acc[j : j + 1, :] = s

        @pl.when(i > 0)
        def _(j=j, s=s):
            acc[j : j + 1, :] += s


def spread(acc, out):
    out[...] = jnp.broadcast_to(acc[...][None], out.shape)


def merge_stats(parts, rows):
    n = parts.shape[0]
    means = parts[:, 0, :]
    mean = jnp.mean(means, axis=0, keepdims=True)
    gaps = means - mean
    dev = jnp.sum(parts[:, 1, :], axis=0, keepdims=True) + rows * jnp.sum(
        gaps * gaps, axis=0, keepdims=True
    )
    return mean, lax.rsqrt(dev * (1.0 / (rows * n)) + EPS)


def exchange(spread_rows):
    return lax.all_to_all(spread_rows, AXES, 0, 0, tiled=True)


def first_kernel(x, gain, bias, w_qkv, w_gate, h1, qkv, z1, stats, acc):
    i = pl.program_id(0)
    ga, bi = row(gain), row(bias)

    def norm(at):
        n, _ = normed(x[at, :].astype(F32))
        h = (n * ga + bi).astype(BF16)
        h1[at, :] = h
        return h

    def multiply(at, h):
        qkv[at, :] = dot(h, w_qkv[...]).astype(BF16)
        z1[at, :] = dot(h, w_gate[...])

    staged(halves_of(x), norm, multiply)
    add_stats(acc, z1[...], i)

    @pl.when(i == pl.num_programs(0) - 1)
    def _():
        spread(acc, stats)


def halves_of(ref):
    return [slice(j, j + HALF) for j in range(0, ref.shape[0], HALF)]


def halo_kernel(x, gain, bias, w_qkv, kv):
    n, _ = normed(x[...].astype(F32))
    h = (n * row(gain) + row(bias)).astype(BF16)
    width = x.shape[1]
    kv[...] = dot(h, w_qkv[:, width:]).astype(BF16)


def attend_kernel(flags, qkv, prev, halo, out, lse, kvp):
    b = pl.program_id(0)
    width = out.shape[1]
    wide = flags[b] > 0

    @pl.when(wide & (b == 0))
    def _():
        kvp[...] = halo[...]

    @pl.when(wide & (b > 0))
    def _():
        kvp[...] = prev[:, width:]

    low = lax.broadcasted_iota(jnp.int32, (1, PAIR), 1) < HD
    keys_at = lax.broadcasted_iota(jnp.int32, (SPAN, SPAN), 0)
    allowed = keys_at <= lax.broadcasted_iota(jnp.int32, (SPAN, SPAN), 1)

    def compute(wide):
        turned = {}

        def scores(p, s):
            q_s = pick_head(qkv[:, p * PAIR : (p + 1) * PAIR], s, low) * jnp.asarray(SCALE, BF16)
            at = slice(width + p * PAIR, width + (p + 1) * PAIR)
            res = [jnp.where(allowed, dot_nt(qkv[:, at], q_s), MASKED)]
            if wide:
                res.append(dot_nt(kvp[:, p * PAIR : (p + 1) * PAIR], q_s))
            return res

        def finish(p, s, res):
            if p not in turned:
                v_at = slice(2 * width + p * PAIR, 2 * width + (p + 1) * PAIR)
                turned[p] = [qkv[:, v_at].T]
                if wide:
                    turned[p].append(kvp[:, width + p * PAIR : width + (p + 1) * PAIR].T)
            top = functools.reduce(
                jnp.maximum, [jnp.max(x, axis=0, keepdims=True) for x in res]
            )
            total, acc = 0.0, 0.0
            for x, vt in zip(res, turned[p]):
                e = jnp.exp(x - top)
                total = total + jnp.sum(e, axis=0, keepdims=True)
                acc = acc + dot(vt[s * HD : (s + 1) * HD], e.astype(BF16))
            lse[p, s : s + 1, :] = top + jnp.log(total)
            return acc * (1.0 / total)

        kept = {}

        def end(unit, res):
            p, s = unit
            kept[s] = finish(p, s, res)
            if s == 1:
                both = jnp.concatenate([kept[0], kept[1]], axis=0)
                out[:, p * PAIR : (p + 1) * PAIR] = both.T.astype(BF16)

        in_turn([(p, s) for p in range(width // PAIR) for s in range(2)], lambda u: scores(*u), end)

    pl.when(wide)(functools.partial(compute, True))
    pl.when(jnp.logical_not(wide))(functools.partial(compute, False))


def pick_head(v, s, low):
    return jnp.where(low if s == 0 else ~low, v, jnp.zeros_like(v))


def staged(units, *stages):
    held = [None] * len(units)
    for t in range(len(units) + len(stages) - 1):
        for k, stage in enumerate(stages):
            if 0 <= t - k < len(units):
                u = t - k
                held[u] = stage(units[u]) if k == 0 else stage(units[u], held[u])


def in_turn(units, first, second):
    held = None
    for u in units:
        got = first(u)
        if held is not None:
            second(*held)
        held = (u, got)
    second(*held)


def mix_kernel(
    rows, att, x, z1, parts, gain, shift, ln_gain, ln_bias, w_out, w_gate, y1, h2, z2, stats, acc, st
):
    i = pl.program_id(0)

    @pl.when(i == 0)
    def _():
        mean, rstd = merge_stats(parts, rows)
        st[0:1, :] = mean
        st[1:2, :] = rstd

    mean, rstd = st[0:1, :], st[1:2, :]
    ga, sh, lg, lb = row(gain), row(shift), row(ln_gain), row(ln_bias)

    def project(at):
        return dot(att[at, :], w_out[...])

    def combine(at, branch):
        t = jax.nn.sigmoid((z1[at, :] - mean) * rstd * ga + sh)
        y = t * branch + (1.0 - t) * x[at, :].astype(F32)
        y1[at, :] = y
        n, _ = normed(y)
        h = (n * lg + lb).astype(BF16)
        h2[at, :] = h
        return h

    def gate(at, h):
        z2[at, :] = dot(h, w_gate[...])

    staged(halves_of(att), project, combine, gate)
    add_stats(acc, z2[...], i)

    @pl.when(i == pl.num_programs(0) - 1)
    def _():
        spread(acc, stats)


GELU_C = 0.7978845608028654
GELU_A = 0.044715


def mlp_kernel(h2, w_up, b_up, w_down, b_down, act, slope, mlp):
    units = w_up.shape[1]
    step = 512
    bias, bias_down = row(b_up), row(b_down)

    def up(u):
        rows, j = u
        at = slice(j * step, (j + 1) * step)
        return dot(h2[rows, :], w_up[:, at])

    def curve(u, pre):
        rows, j = u
        at = slice(j * step, (j + 1) * step)
        pre = pre + bias[:, at]
        bend = GELU_C + (GELU_C * GELU_A) * (pre * pre)
        half = 0.5 * jnp.tanh(pre * bend)
        cdf = 0.5 + half
        a = pre * cdf
        act[rows, at] = a.astype(BF16)
        slope[rows, at] = (cdf + a * (0.5 - half) * (6.0 * bend - 4.0 * GELU_C)).astype(BF16)

    def down(u, _):
        rows, j = u
        if j == units // step - 1:
            mlp[rows, :] = dot(act[rows, :], w_down[...]) + bias_down

    staged([(r, j) for r in halves_of(h2) for j in range(units // step)], up, curve, down)


def gate2_kernel(rows, mlp, y1, z2, c, parts, gain, shift, out, dmlp, sums, acc, st):
    i = pl.program_id(0)

    @pl.when(i == 0)
    def _():
        mean, rstd = merge_stats(parts, rows)
        st[0:1, :] = mean
        st[1:2, :] = rstd

    nhat = (z2[...] - st[0:1, :]) * st[1:2, :]
    t = jax.nn.sigmoid(nhat * row(gain) + row(shift))
    m, y = mlp[...], y1[...]
    out[...] = (t * m + (1.0 - t) * y).astype(BF16)
    g = c[...].astype(F32)
    dmlp[...] = (g * t).astype(BF16)
    du = g * (m - y) * t * (1.0 - t)
    add_sums(acc, [column_sum(du), column_sum(du * nhat)], i)

    @pl.when(i == pl.num_programs(0) - 1)
    def _():
        spread(acc, sums)


def mlp_back_kernel(
    core, dmlp, act, slope, h2, w_up, w_down, dh2, keep, send, g_b, acc_up, acc_down
):
    i = pl.program_id(0)

    @pl.when(i == 0)
    def _():
        acc_up[...] = jnp.zeros_like(acc_up)
        acc_down[...] = jnp.zeros_like(acc_down)
        g_b[...] = jnp.zeros_like(g_b)

    d, h = dmlp[...], h2[...]
    units = w_up.shape[1]
    total = 0.0
    width = d.shape[1]
    steps = units // width
    for j in range(steps):
        at = slice(j * width, (j + 1) * width)
        dp = (dot_nt(d, w_down[at, :]) * slope[:, at].astype(F32)).astype(BF16)
        g_b[1 + j : 2 + j, :] += column_sum(dp.astype(F32))
        total = total + dot_nt(dp, w_up[:, at])
        acc_up[at, :] += dot_tn(h, dp)
        acc_down[:, at] += dot_tn(d, act[:, at])
    dh2[...] = total
    g_b[0:1, :] += column_sum(d.astype(F32))

    @pl.when(i == pl.num_programs(0) - 1)
    def _():
        for j in range(steps):
            at = slice(j * width, (j + 1) * width)
            half, row0 = (2 * j) // steps, (j % (steps // 2)) * width
            to = slice(row0, row0 + width)
            for out, mine in ((keep, core[0] == half), (send, core[0] != half)):

                @pl.when(mine)
                def _(out=out, at=at, to=to):
                    out[0, to, :] = acc_up[at, :].astype(BF16)
                    out[1, to, :] = acc_down[:, at].T.astype(BF16)


def middle_kernel(
    rows,
    c,
    mlp,
    y1,
    z2,
    dh2p,
    att,
    x,
    z1,
    h2,
    parts2,
    sums2,
    parts1,
    gain2,
    shift2,
    gain1,
    shift1,
    ln_gain,
    g_b,
    w_gate2,
    w_out,
    gx,
    du1,
    datt,
    delta,
    g_w,
    sums,
    g_gate2,
    side,
    acc,
    st,
    acc_gate,
    acc_out,
):
    i = pl.program_id(0)
    count = 1.0 / (rows * parts2.shape[0])
    width = y1.shape[1]

    @pl.when(i == 0)
    def _():
        mean, rstd = merge_stats(parts2, rows)
        st[0:1, :] = mean
        st[1:2, :] = rstd
        mean, rstd = merge_stats(parts1, rows)
        st[2:3, :] = mean
        st[3:4, :] = rstd
        st[4:5, :] = jnp.sum(sums2[:, 0, :], axis=0, keepdims=True)
        st[5:6, :] = jnp.sum(sums2[:, 1, :], axis=0, keepdims=True)
        g_gate2[...] = st[4:6, :]
        acc_gate[...] = jnp.zeros_like(acc_gate)
        acc_out[...] = jnp.zeros_like(acc_out)

    g = c[...].astype(F32)
    y = y1[...]
    nhat2 = (z2[...] - st[0:1, :]) * st[1:2, :]
    t2 = jax.nn.sigmoid(nhat2 * row(gain2) + row(shift2))
    du2 = g * (mlp[...] - y) * t2 * (1.0 - t2)
    dz2 = (
        (row(gain2) * st[1:2, :]) * (du2 - st[4:5, :] * count - nhat2 * (st[5:6, :] * count))
    ).astype(BF16)
    acc_gate[...] += dot_tn(h2[...], dz2)
    dh2 = dh2p[...] + dot_nt(dz2, w_gate2[...])
    n, r = normed(y)
    e = dh2 * row(ln_gain)
    dy = g * (1.0 - t2) + r * (
        e - jnp.mean(e, axis=-1, keepdims=True) - n * jnp.mean(e * n, axis=-1, keepdims=True)
    )
    a = att[...]
    branch = dot(a, w_out[...])
    nhat1 = (z1[...] - st[2:3, :]) * st[3:4, :]
    t1 = jax.nn.sigmoid(nhat1 * row(gain1) + row(shift1))
    dbranch = (dy * t1).astype(BF16)
    gx[...] = dy * (1.0 - t1)
    du = dy * (branch - x[...].astype(F32)) * t1 * (1.0 - t1)
    du1[...] = du
    acc_out[...] += dot_tn(a, dbranch)
    da = dot_nt(dbranch, w_out[...]).astype(BF16)
    datt[...] = da
    prod = da.astype(F32) * a.astype(F32)
    hi = prod.astype(BF16)
    lo = (prod - hi.astype(F32)).astype(BF16)
    heads = width // HD
    pick = (
        lax.broadcasted_iota(jnp.int32, (heads, width), 1) // HD
        == lax.broadcasted_iota(jnp.int32, (heads, width), 0)
    ).astype(BF16)
    dl = dot_nt(pick, hi) + dot_nt(pick, lo)
    for p in range(heads // 2):
        delta[p] = dl[2 * p : 2 * p + 2, :]
    add_sums(
        acc, [column_sum(du), column_sum(du * nhat1), column_sum(dh2 * n), column_sum(dh2)], i
    )

    @pl.when(i == pl.num_programs(0) - 1)
    def _():
        spread(acc.at[0:2, :], sums)
        side[0:2, :] = acc[2:4, :]
        side[2:, :] = g_b[...]
        g_w[0] = acc_gate[...].astype(BF16)
        g_w[1] = acc_out[...].astype(BF16)


def back_block(q_ref, k_ref, v_ref, do, lse, delta, kp_ref, vp_ref, wide, own, carry, dq_t):
    width = do.shape[1]
    low = lax.broadcasted_iota(jnp.int32, (1, PAIR), 1) < HD
    mask = lax.broadcasted_iota(jnp.int32, (HALF, HALF), 0) <= lax.broadcasted_iota(
        jnp.int32, (HALF, HALF), 1
    )
    full = slice(0, SPAN)
    parts = [(slice(0, HALF), full), (slice(HALF, SPAN), slice(HALF, SPAN))]
    units = []
    for p in range(width // PAIR):
        for s in range(2):
            units += [(p, s, 0), (p, s, 1)] + ([(p, s, 2)] if wide else [])
    held = {}

    def inputs(p):
        if p not in held:
            held.clear()
            at = slice(p * PAIR, (p + 1) * PAIR)
            q, d, k, v = q_ref[:, at], do[:, at], k_ref[:, at], v_ref[:, at]
            scale = jnp.asarray(SCALE, BF16)
            e = {
                "q": [pick_head(q, s, low) * scale for s in range(2)],
                "do": [pick_head(d, s, low) for s in range(2)],
                "own": (k, v, k.T * scale),
            }
            if wide:
                kp, vp = kp_ref[:, at], vp_ref[:, at]
                e["before"] = (kp, vp, kp.T * scale)
            held[p] = e
        return held[p]

    def first(unit):
        p, s, i = unit
        e = inputs(p)
        ks, qs = (full, full) if i == 2 else parts[i]
        k, v, kt = e["before"] if i == 2 else e["own"]
        q_s, d_s = e["q"][s][qs], e["do"][s][qs]
        kt = kt[s * HD : (s + 1) * HD, ks]
        return dot_nt(k[ks], q_s), dot_nt(v[ks], d_s), q_s, d_s, kt, ks, qs

    def second(unit, got):
        p, s, i = unit
        scores, dp, q_s, d_s, kt, ks, qs = got
        at = slice(p * PAIR, (p + 1) * PAIR)
        x = jnp.exp(scores - lse[p, s : s + 1, qs])
        if i == 0:
            x = jnp.concatenate([jnp.where(mask, x[:, :HALF], 0.0), x[:, HALF:]], axis=1)
        elif i == 1:
            x = jnp.where(mask, x, 0.0)
        ds = (x * (dp - delta[p, s : s + 1, qs])).astype(BF16)
        dk, dv, dq = dot(ds, q_s), dot(x.astype(BF16), d_s), dot(kt, ds)
        target = carry if i == 2 else own
        if s == 0:
            target[0, ks, at] = dk
            target[1, ks, at] = dv
        else:
            target[0, ks, at] += dk
            target[1, ks, at] += dv
        head = slice(p * PAIR + s * HD, p * PAIR + (s + 1) * HD)
        if i == 0:
            dq_t[head, :] = dq
        else:
            dq_t[head, qs] += dq

    in_turn(units, first, second)


def back_first_kernel(flags, q, k, v, do, kp, vp, lse, delta, dq, own, terms, dq_t, carry):
    wide = flags[0] > 0

    @pl.when(wide)
    def _():
        back_block(q, k, v, do, lse, delta, kp, vp, True, own, carry, dq_t)
        terms[...] = carry[...].astype(BF16)

    @pl.when(jnp.logical_not(wide))
    def _():
        back_block(q, k, v, do, lse, delta, kp, vp, False, own, carry, dq_t)
        terms[...] = jnp.zeros_like(terms)

    dq[...] = dq_t[...].T.astype(BF16)


def back_rest_kernel(
    flags, q, k, v, do, kp, vp, lse, delta, dq0, own0, dq, dk, dv, last, dq_t, carry, own
):
    j = pl.program_id(0)
    b = pl.num_programs(0) - 1 - j
    now = lax.rem(j, 2)

    @pl.when(b > 0)
    def _():
        later = carry.at[1 - now]
        wide = flags[b] > 0

        @pl.when(wide)
        def _():
            back_block(q, k, v, do, lse, delta, kp, vp, True, own, later, dq_t)

        @pl.when(jnp.logical_not(wide))
        def _():
            back_block(q, k, v, do, lse, delta, kp, vp, False, own, later, dq_t)
            later[...] = jnp.zeros_like(later)

        @pl.when(j == 0)
        def _():
            last[...] = own[...]

        @pl.when(j > 0)
        def _():
            dk[...] = (own[0] + carry[now, 0]).astype(BF16)
            dv[...] = (own[1] + carry[now, 1]).astype(BF16)

        dq[...] = dq_t[...].T.astype(BF16)

    @pl.when(b == 0)
    def _():
        dq[...] = dq0[...]
        dk[...] = (own0[0] + carry[now, 0]).astype(BF16)
        dv[...] = (own0[1] + carry[now, 1]).astype(BF16)


def last_kernel(
    rows,
    core,
    h1,
    dq_a,
    dk_a,
    dv_a,
    last_a,
    dq_b,
    dk_b,
    dv_b,
    last_b,
    arrived,
    du1,
    z1,
    parts1,
    sums1,
    gain1,
    g_mid,
    side,
    x,
    gx,
    ln_gain,
    w_qkv,
    w_gate1,
    grad_x,
    keep,
    send,
    g_sums,
    acc,
    st,
    dqkv,
    ln_sums,
):
    i = pl.program_id(0)
    final = i == pl.num_programs(0) - 1
    count = 1.0 / (rows * parts1.shape[0])
    width = h1.shape[1]

    @pl.when(i == 0)
    def _():
        mean, rstd = merge_stats(parts1, rows)
        st[2:3, :] = mean
        st[3:4, :] = rstd
        for j in range(sums1.shape[1]):
            g_sums[j : j + 1, :] = jnp.sum(sums1[:, j, :], axis=0, keepdims=True)
        acc[...] = jnp.zeros_like(acc)

    nhat = (z1[...] - st[2:3, :]) * st[3:4, :]
    dz = (
        (row(gain1) * st[3:4, :])
        * (du1[...] - g_sums[0:1, :] * count - nhat * (g_sums[1:2, :] * count))
    ).astype(BF16)

    half = dq_a.shape[1]
    dqkv[:, :half] = dq_a[...]
    dqkv[:, half:width] = dq_b[...]

    @pl.when(jnp.logical_not(final))
    def _():
        dqkv[:, width : width + half] = dk_a[...]
        dqkv[:, width + half : 2 * width] = dk_b[...]
        dqkv[:, 2 * width : 2 * width + half] = dv_a[...]
        dqkv[:, 2 * width + half :] = dv_b[...]

    @pl.when(final)
    def _():
        for j in range(2):
            for c, own in enumerate((last_a, last_b)):
                got = arrived[j, :, c * half : (c + 1) * half].astype(F32)
                at = (1 + j) * width + c * half
                dqkv[:, at : at + half] = (own[j] + got).astype(BF16)

    ht = h1[...].T
    for j in range(3):
        acc[j] += dot(ht, dqkv[:, j * width : (j + 1) * width])
    acc[3] += dot(ht, dz)
    dh = dot_nt(dqkv[...], w_qkv[...]) + dot_nt(dz, w_gate1[...])
    n, r = normed(x[...].astype(F32))
    e = dh * row(ln_gain)
    grad_x[...] = gx[...] + r * (
        e - jnp.mean(e, axis=-1, keepdims=True) - n * jnp.mean(e * n, axis=-1, keepdims=True)
    )
    add_sums(ln_sums, [column_sum(dh * n), column_sum(dh)], i)

    @pl.when(final)
    def _():
        mine, other = pl.ds(core[0] * HALF, HALF), pl.ds((1 - core[0]) * HALF, HALF)
        for out, at in ((keep, mine), (send, other)):
            for j in range(4):
                out[j // 2, (j % 2) * HALF : (j % 2 + 1) * HALF, :] = acc[j, at, :].astype(BF16)
            for j in range(2):
                out[j, 2 * HALF : 3 * HALF, :] = g_mid[j, at, :]
                out[j, 3 * HALF :, :] = jnp.zeros((PAD, width), BF16)
        extra = side.shape[0]
        for out, mine in ((keep, core[0] == 0), (send, core[0] != 0)):

            @pl.when(mine)
            def _(out=out):
                out[0, 3 * HALF : 3 * HALF + 16, :] = jnp.concatenate(
                    [ln_sums[...], side[...], jnp.zeros((14 - extra, width), F32)], axis=0
                ).astype(BF16)


def between_chips(x):
    seq, head = lax.axis_size("seq"), lax.axis_size("head")
    groups = [[d for d in range(seq * head) if (d // head) % 2 == c] for c in range(2)]
    return lax.all_to_all(x, AXES, 0, 0, axis_index_groups=groups, tiled=True)


def swap(x, axis, bit):
    n = lax.axis_size(axis)
    return lax.ppermute(x, axis, [(i, i ^ bit) for i in range(n)])


def upper(axis, bit):
    return (lax.axis_index(axis) & bit) // bit


def bits(axis):
    return [(axis, 1 << j) for j in range((lax.axis_size(axis) - 1).bit_length())]


class Total:
    def __init__(self, keep, send):
        near = bits("seq")
        first, layer, far = near[:1], near[1:], bits("head")
        self.orders = [first + layer + far, first + layer[::-1] + far]
        self.steps = len(self.orders[0])
        self.keep = [keep[0], keep[1]]
        self.send = send
        self.got = None
        self.at = 0

    def _swap(self, parts, stage):
        a, b = self.orders[0][stage], self.orders[1][stage]
        if a == b:
            both = swap(jnp.stack(parts) if isinstance(parts, list) else parts, *a)
            return [both[0], both[1]]
        return [swap(parts[0], *a), swap(parts[1], *b)]

    def _sum(self, lane, stage, up):
        keep, got = self.keep[lane], self.got[lane]
        half = keep.shape[0] // 2
        mine = upper(*self.orders[lane][stage])
        start = (mine if up else 1 - mine) * half
        a = lax.dynamic_slice_in_dim(keep, start, half, 0)
        b = lax.dynamic_slice_in_dim(got, start, half, 0)
        return (a.astype(F32) + b.astype(F32)).astype(BF16)

    def left(self):
        return 2 * self.steps - self.at

    def parts(self):
        k, n = self.at, self.steps
        if k == 0:
            return self.send
        if k < n:
            parts = [self._sum(lane, k, False) for lane in range(2)]
            self.keep = [self._sum(lane, k, True) for lane in range(2)]
            return parts
        if k == n:
            self.keep = [
                (a.astype(F32) + b.astype(F32)).astype(BF16) for a, b in zip(self.keep, self.got)
            ]
        else:
            self.keep = self._joined(2 * n - k)
        return self.keep

    def start(self, parts):
        k, n = self.at, self.steps
        if k >= n:
            self.keep = parts
        self.got = self._swap(parts, k if k < n else 2 * n - 1 - k)
        self.at += 1

    def _joined(self, stage):
        out = []
        for lane in range(2):
            up = upper(*self.orders[lane][stage]) > 0
            a, b = self.keep[lane], self.got[lane]
            out.append(jnp.concatenate([jnp.where(up, b, a), jnp.where(up, a, b)], axis=0))
        return out

    def result(self):
        return [v.astype(F32) for v in self._joined(0)]


def joint_step(totals, held=()):
    parts, held = lax.optimization_barrier(([t.parts() for t in totals], held))
    for t, p in zip(totals, parts):
        t.start(p)
    return held


def continuation(lengths, span):
    place = jnp.arange(lengths.shape[0], dtype=jnp.int32)
    starts = jnp.sum(jnp.where(place[None, :] < place[:, None], lengths[None, :], 0), axis=1)
    begins = place * span
    hit = (starts[None, :] == begins[:, None]) & (lengths[None, :] > 0)
    return 1 - jnp.max(hit.astype(jnp.int32), axis=1)


def body(
    tokens,
    seq_lengths,
    ln1_gain,
    ln1_bias,
    w_qkv,
    w_out,
    w_gate1,
    gate1_gain,
    gate1_shift,
    ln2_gain,
    ln2_bias,
    w_up,
    b_up,
    w_down,
    b_down,
    w_gate2,
    gate2_gain,
    gate2_shift,
    cotangent,
):
    rows, width = tokens.shape
    units = w_up.shape[1]
    ndev = lax.axis_size("seq") * lax.axis_size("head")
    blocks = rows // SPAN
    pairs = width // PAIR
    heads = width // HD
    count = lax.axis_size("head")
    mac = rows * width * width

    tail = tokens[rows - SPAN :]
    before = lax.ppermute(tail, "head", [(i, i + 1) for i in range(count - 1)])
    flags = lax.dynamic_slice_in_dim(
        continuation(seq_lengths[0], SPAN), lax.axis_index("head") * blocks, blocks, 0
    )

    vec = whole((width,))
    stats_shape = (ndev, 2, width)
    h1, qkv, z1, stats1 = pl.pallas_call(
        first_kernel,
        grid=(blocks,),
        in_specs=[rows_of(width), vec, vec, whole(w_qkv.shape), whole(w_gate1.shape)],
        out_specs=[rows_of(width), rows_of(3 * width), rows_of(width), whole(stats_shape)],
        out_shape=[
            struct((rows, width), BF16),
            struct((rows, 3 * width), BF16),
            struct((rows, width), F32),
            struct(stats_shape, F32),
        ],
        scratch_shapes=[pltpu.VMEM((2, width), F32)],
        compiler_params=params(VMEM_MIB),
        cost_estimate=cost(8 * mac, rows * width * 14, rows),
        name="first",
    )(tokens, ln1_gain, ln1_bias, w_qkv, w_gate1)
    parts1 = exchange(stats1)

    kv_halo = pl.pallas_call(
        halo_kernel,
        out_shape=struct((SPAN, 2 * width), BF16),
        compiler_params=pltpu.CompilerParams(vmem_limit_bytes=VMEM_MIB * MIB),
        cost_estimate=cost(4 * SPAN * width * width, 4 * MIB, SPAN),
        name="halo",
    )(before, ln1_gain, ln1_bias, w_qkv)

    att, lse = pl.pallas_call(
        attend_kernel,
        grid_spec=pltpu.PrefetchScalarGridSpec(
            num_scalar_prefetch=1,
            grid=(blocks,),
            in_specs=[
                pl.BlockSpec((SPAN, 3 * width), lambda b, f: (b, 0)),
                pl.BlockSpec((SPAN, 3 * width), lambda b, f: (jnp.maximum(b - 1, 0), 0)),
                whole((SPAN, 2 * width)),
            ],
            out_specs=[
                pl.BlockSpec((SPAN, width), lambda b, f: (b, 0)),
                pl.BlockSpec((pairs, 2, SPAN), lambda b, f: (0, 0, b)),
            ],
            scratch_shapes=[pltpu.VMEM((SPAN, 2 * width), BF16)],
        ),
        out_shape=[struct((rows, width), BF16), struct((pairs, 2, rows), F32)],
        compiler_params=params(VMEM_MIB),
        cost_estimate=cost(10 * heads * SPAN * SPAN * PAIR * 4, 12 * MIB, heads * SPAN * SPAN * 5),
        name="attend",
    )(flags, qkv, qkv, kv_halo)

    y1, h2, z2, stats2 = pl.pallas_call(
        functools.partial(mix_kernel, rows),
        grid=(blocks,),
        in_specs=[rows_of(width), rows_of(width), rows_of(width), whole(stats_shape)]
        + [vec] * 4
        + [whole(w_out.shape), whole(w_gate2.shape)],
        out_specs=[rows_of(width), rows_of(width), rows_of(width), whole(stats_shape)],
        out_shape=[
            struct((rows, width), F32),
            struct((rows, width), BF16),
            struct((rows, width), F32),
            struct(stats_shape, F32),
        ],
        scratch_shapes=[pltpu.VMEM((2, width), F32), pltpu.VMEM((8, width), F32)],
        compiler_params=params(VMEM_MIB),
        cost_estimate=cost(4 * mac, rows * width * 18, rows * width),
        name="mix",
    )(att, tokens, z1, parts1, gate1_gain, gate1_shift, ln2_gain, ln2_bias, w_out, w_gate2)
    parts2 = exchange(stats2)

    act, slope, mlp = pl.pallas_call(
        mlp_kernel,
        grid=(blocks,),
        in_specs=[
            rows_of(width),
            whole(w_up.shape),
            whole((units,)),
            whole(w_down.shape),
            vec,
        ],
        out_specs=[rows_of(units), rows_of(units), rows_of(width)],
        out_shape=[
            struct((rows, units), BF16),
            struct((rows, units), BF16),
            struct((rows, width), F32),
        ],
        compiler_params=params(VMEM_MIB),
        cost_estimate=cost(4 * rows * width * units, rows * units * 4, rows * units),
        name="mlp",
    )(h2, w_up, b_up, w_down, b_down)

    output, dmlp, sums2 = pl.pallas_call(
        functools.partial(gate2_kernel, rows),
        grid=(blocks,),
        in_specs=[rows_of(width)] * 4 + [whole(stats_shape), vec, vec],
        out_specs=[rows_of(width), rows_of(width), whole(stats_shape)],
        out_shape=[
            struct((rows, width), BF16),
            struct((rows, width), BF16),
            struct(stats_shape, F32),
        ],
        scratch_shapes=[pltpu.VMEM((2, width), F32), pltpu.VMEM((8, width), F32)],
        compiler_params=params(VMEM_MIB),
        cost_estimate=cost(rows * width * 20, rows * width * 18, rows * width),
        name="gate2",
    )(mlp, y1, z2, cotangent, parts2, gate2_gain, gate2_shift)
    parts_du2 = exchange(sums2)

    bias_rows = 1 + units // width
    core = (lax.axis_index("seq") & 1).reshape(1)
    smem = pl.BlockSpec(memory_space=pltpu.SMEM)
    mlp_half = (2, units // 2, width)
    dh2p, keep, send, g_b = pl.pallas_call(
        mlp_back_kernel,
        grid=(blocks,),
        in_specs=[
            smem,
            rows_of(width),
            rows_of(units),
            rows_of(units),
            rows_of(width),
            whole(w_up.shape),
            whole(w_down.shape),
        ],
        out_specs=[
            rows_of(width),
            whole(mlp_half),
            whole(mlp_half),
            whole((bias_rows, width)),
        ],
        out_shape=[
            struct((rows, width), F32),
            struct(mlp_half, BF16),
            struct(mlp_half, BF16),
            struct((bias_rows, width), F32),
        ],
        scratch_shapes=[pltpu.VMEM((units, width), F32), pltpu.VMEM((width, units), F32)],
        compiler_params=params(VMEM_MIB),
        cost_estimate=cost(8 * rows * width * units, rows * units * 5),
        name="mlp_back",
    )(core, dmlp, act, slope, h2, w_up, w_down)
    keep, send, dh2p, parts_du2 = lax.optimization_barrier((keep, send, dh2p, parts_du2))
    swapped = swap(send, "seq", 1)
    chips = ndev // 2
    pair_sum = (keep.astype(F32) + swapped.astype(F32)).astype(BF16)
    pair_sum = pair_sum.reshape(chips, units // chips, width)
    pair_sum, dh2p = lax.optimization_barrier((pair_sum, dh2p))
    scattered = between_chips(pair_sum)

    mid_shape = (2, width, width)
    rows_pair = pl.BlockSpec((pairs, 2, SPAN), lambda i: (0, 0, i))
    side_rows = 2 + bias_rows
    gx, du1, datt, delta, g_mid, sums1, g_gate2, side = pl.pallas_call(
        functools.partial(middle_kernel, rows),
        grid=(blocks,),
        in_specs=[rows_of(width)] * 9
        + [whole(stats_shape)] * 3
        + [vec] * 5
        + [whole((bias_rows, width)), whole(w_gate2.shape), whole(w_out.shape)],
        out_specs=[
            rows_of(width),
            rows_of(width),
            rows_of(width),
            rows_pair,
            whole(mid_shape),
            whole(stats_shape),
            whole((2, width)),
            whole((side_rows, width)),
        ],
        out_shape=[
            struct((rows, width), F32),
            struct((rows, width), F32),
            struct((rows, width), BF16),
            struct((pairs, 2, rows), F32),
            struct(mid_shape, BF16),
            struct(stats_shape, F32),
            struct((2, width), F32),
            struct((side_rows, width), F32),
        ],
        scratch_shapes=[
            pltpu.VMEM((4, width), F32),
            pltpu.VMEM((8, width), F32),
            pltpu.VMEM((width, width), F32),
            pltpu.VMEM((width, width), F32),
        ],
        compiler_params=params(VMEM_MIB),
        cost_estimate=cost(10 * mac, rows * width * 38, rows * width * 2),
        name="middle",
    )(
        cotangent,
        mlp,
        y1,
        z2,
        dh2p,
        att,
        tokens,
        z1,
        h2,
        parts2,
        parts_du2,
        parts1,
        gate2_gain,
        gate2_shift,
        gate1_gain,
        gate1_shift,
        ln2_gain,
        g_b,
        w_gate2,
        w_out,
    )

    def columns_at(j, parts=1):
        return lambda i, f: (0, j * parts)

    dq0, own0, terms = pl.pallas_call(
        back_first_kernel,
        grid_spec=pltpu.PrefetchScalarGridSpec(
            num_scalar_prefetch=1,
            grid=(1,),
            in_specs=[
                pl.BlockSpec((SPAN, width), columns_at(0)),
                pl.BlockSpec((SPAN, width), columns_at(1)),
                pl.BlockSpec((SPAN, width), columns_at(2)),
                whole((SPAN, width)),
                pl.BlockSpec((SPAN, width), columns_at(0)),
                pl.BlockSpec((SPAN, width), columns_at(1)),
                whole((pairs, 2, SPAN)),
                whole((pairs, 2, SPAN)),
            ],
            out_specs=[
                whole((SPAN, width)),
                whole((2, SPAN, width)),
                whole((2, SPAN, width)),
            ],
            scratch_shapes=[
                pltpu.VMEM((width, SPAN), F32),
                pltpu.VMEM((2, SPAN, width), F32),
            ],
        ),
        out_shape=[
            struct((SPAN, width), BF16),
            struct((2, SPAN, width), F32),
            struct((2, SPAN, width), BF16),
        ],
        compiler_params=params(VMEM_MIB),
        cost_estimate=cost(
            10 * heads * SPAN * SPAN * PAIR * 2, 8 * MIB, heads * SPAN * SPAN * 2
        ),
        name="attend_back_first",
    )(flags, qkv, qkv, qkv, datt, kv_halo, kv_halo, lse, delta)
    arrived = lax.ppermute(terms, "head", [(i + 1, i) for i in range(count - 1)])

    def block(j):
        return jnp.maximum(blocks - 1 - j, 1)

    groups = 2
    group = width // groups

    def back_rest(g, own0, weight):
        def at(column, shift=0):
            return pl.BlockSpec(
                (SPAN, group), lambda j, f: (block(j) - shift, column * groups + g)
            )

        row_block = pl.BlockSpec((pairs // groups, 2, SPAN), lambda j, f: (g, 0, block(j)))
        out_block = pl.BlockSpec((SPAN, group), lambda j, f: (blocks - 1 - j, 0))
        return pl.pallas_call(
            back_rest_kernel,
            grid_spec=pltpu.PrefetchScalarGridSpec(
                num_scalar_prefetch=1,
                grid=(blocks,),
                in_specs=[
                    at(0),
                    at(1),
                    at(2),
                    at(0),
                    at(1, 1),
                    at(2, 1),
                    row_block,
                    row_block,
                    pl.BlockSpec((SPAN, group), lambda j, f: (0, g)),
                    pl.BlockSpec((2, SPAN, group), lambda j, f: (0, 0, g)),
                ],
                out_specs=[out_block, out_block, out_block, whole((2, SPAN, group))],
                scratch_shapes=[
                    pltpu.VMEM((group, SPAN), F32),
                    pltpu.VMEM((2, 2, SPAN, group), F32),
                    pltpu.VMEM((2, SPAN, group), F32),
                ],
            ),
            out_shape=[struct((rows, group), BF16)] * 3 + [struct((2, SPAN, group), F32)],
            compiler_params=params(VMEM_MIB),
            cost_estimate=cost(
                10 * weight * heads * SPAN * SPAN * PAIR * 3,
                10 * weight * MIB,
                weight * heads * SPAN * SPAN * 2,
            ),
            name="attend_back_rest",
        )(flags, qkv, qkv, qkv, datt, qkv, qkv, lse, delta, dq0, own0)

    back_a = back_rest(0, own0, 1.0)
    back_a, scattered = lax.optimization_barrier((back_a, scattered))
    mine = jnp.sum(scattered.astype(F32), axis=0).astype(BF16)
    mine = jnp.broadcast_to(mine[None], pair_sum.shape)
    mine, own0, sums1 = lax.optimization_barrier((mine, own0, sums1))
    parts_du1 = exchange(sums1)
    back_b = back_rest(1, own0, LATE_WEIGHT)
    mine, parts_du1, back_b, arrived = lax.optimization_barrier((mine, parts_du1, back_b, arrived))
    gathered = between_chips(mine)

    in_half = (2, 3 * HALF + PAD, width)
    grouped = [rows_of(group)] * 3 + [whole((2, SPAN, group))]
    grad_x, keep, send, g_sums = pl.pallas_call(
        functools.partial(last_kernel, rows),
        grid=(blocks,),
        in_specs=[smem, rows_of(width)]
        + grouped * 2
        + [whole((2, SPAN, width))]
        + [rows_of(width)] * 2
        + [whole(stats_shape), whole(stats_shape), vec, whole(mid_shape)]
        + [whole((side_rows, width))]
        + [rows_of(width)] * 2
        + [vec, whole(w_qkv.shape), whole(w_gate1.shape)],
        out_specs=[
            rows_of(width),
            whole(in_half),
            whole(in_half),
            whole((2, width)),
        ],
        out_shape=[
            struct((rows, width), F32),
            struct(in_half, BF16),
            struct(in_half, BF16),
            struct((2, width), F32),
        ],
        scratch_shapes=[
            pltpu.VMEM((4, width, width), F32),
            pltpu.VMEM((8, width), F32),
            pltpu.VMEM((SPAN, 3 * width), BF16),
            pltpu.VMEM((2, width), F32),
        ],
        compiler_params=params(VMEM_MIB),
        cost_estimate=cost(LATE_WEIGHT * 16 * mac, LATE_WEIGHT * rows * width * 26),
        name="last",
    )(
        core,
        h1,
        *back_a,
        *back_b,
        arrived,
        du1,
        z1,
        parts1,
        parts_du1,
        gate1_gain,
        g_mid,
        side,
        tokens,
        gx,
        ln1_gain,
        w_qkv,
        w_gate1,
    )

    total = Total(keep, send)
    while total.left() > total.steps + 2:
        joint_step([total])
    gathered = joint_step([total], gathered)
    joint_step([total])
    gathered = gathered.reshape(mlp_half)
    other = swap(gathered, "seq", 1)
    up = upper("seq", 1) > 0
    other, gathered = joint_step([total], (other, gathered))
    g_up, g_down = [
        jnp.concatenate([jnp.where(up, b, a), jnp.where(up, a, b)], axis=0).astype(F32)
        for a, b in zip(gathered, other)
    ]
    g_up = g_up.reshape(units // width, width, width).transpose(1, 0, 2).reshape(width, units)
    g_up = joint_step([total], g_up)
    g_down = joint_step([total], g_down)
    while total.left():
        joint_step([total])
    sums_a, sums_b = [v.reshape(2, 3 * HALF + PAD, width) for v in total.result()]
    ln_b = sums_a[0, 3 * HALF : 3 * HALF + 2 + side_rows]
    halves = [v[:, : 3 * HALF].reshape(2, 3, HALF, width) for v in (sums_a, sums_b)]

    def block_of(lane, j):
        return jnp.concatenate([halves[lane][0, j], halves[lane][1, j]], axis=0)

    g_qkv = jnp.concatenate([block_of(0, 0), block_of(0, 1), block_of(1, 0)], axis=1)
    return (
        output,
        grad_x,
        ln_b[0],
        ln_b[1],
        g_qkv,
        block_of(1, 2),
        block_of(1, 1),
        g_sums[1],
        g_sums[0],
        ln_b[2],
        ln_b[3],
        g_up,
        ln_b[5:].reshape(units),
        g_down,
        ln_b[4],
        block_of(0, 2),
        g_gate2[1],
        g_gate2[0],
    )


def solution(mesh):
    split = P(AXES, None)
    return jax.shard_map(
        body,
        mesh=mesh,
        in_specs=(split, P("seq", None)) + (P(),) * 16 + (split,),
        out_specs=(split, split) + (P(),) * 16,
        check_vma=False,
    )
```

```python
import functools

import jax
import jax.numpy as jnp
from jax import lax
from jax.experimental import pallas as pl
from jax.experimental.pallas import tpu as pltpu
from jax.sharding import PartitionSpec as P

HD = 64
SPAN = 512
TILE = 1024
MID_TILE = 512
HALF = 256
PAIR = 128
PAD = 128
LATE_WEIGHT = 0.02
EPS = 1e-05
MASKED = -1e30
SCALE = 0.125
AXES = ("seq", "head")
MIB = 1024 * 1024
VMEM_MIB = 60

F32 = jnp.float32
BF16 = jnp.bfloat16


def dot(a, b):
    return jnp.dot(a, b, preferred_element_type=F32)


def dot_nt(a, b):
    return lax.dot_general(a, b, (((1,), (1,)), ((), ())), preferred_element_type=F32)


def dot_tn(a, b):
    return lax.dot_general(a, b, (((0,), (0,)), ((), ())), preferred_element_type=F32)


def struct(shape, dtype):
    return jax.ShapeDtypeStruct(shape, dtype)


def params(mib):
    return pltpu.CompilerParams(vmem_limit_bytes=mib * MIB, dimension_semantics=("arbitrary",))


def cost(flops, nbytes, trans=0):
    return pl.CostEstimate(flops=int(flops), bytes_accessed=int(nbytes), transcendentals=int(trans))


def rows_of(width, tile=TILE):
    return pl.BlockSpec((tile, width), lambda i: (i, 0))


def whole(shape):
    return pl.BlockSpec(shape, lambda *_: (0,) * len(shape))


def normed(v):
    centered = v - jnp.mean(v, axis=-1, keepdims=True)
    rstd = lax.rsqrt(jnp.mean(centered * centered, axis=-1, keepdims=True) + EPS)
    return centered * rstd, rstd


def row(ref):
    return ref[...].reshape(1, -1)


def sigmoid(v):
    return 0.5 + 0.5 * jnp.tanh(0.5 * v)


def column_sum(v):
    return jnp.sum(v, axis=0, keepdims=True)


def add_stats(acc, z, i):
    n = z.shape[0]
    mean = column_sum(z) * (1.0 / n)
    c = z - mean
    dev = column_sum(c * c)

    @pl.when(i == 0)
    def _():
        acc[0:1, :] = mean
        acc[1:2, :] = dev

    @pl.when(i > 0)
    def _():
        before = i.astype(F32)
        gap = mean - acc[0:1, :]
        acc[0:1, :] += gap / (before + 1.0)
        acc[1:2, :] += dev + gap * gap * (n * before / (before + 1.0))


def add_sums(acc, sums, i):
    for j, s in enumerate(sums):

        @pl.when(i == 0)
        def _(j=j, s=s):
            acc[j : j + 1, :] = s

        @pl.when(i > 0)
        def _(j=j, s=s):
            acc[j : j + 1, :] += s


def spread(acc, out):
    out[...] = jnp.broadcast_to(acc[...][None], out.shape)


def merge_stats(parts, rows):
    n = parts.shape[0]
    means = parts[:, 0, :]
    mean = jnp.mean(means, axis=0, keepdims=True)
    gaps = means - mean
    dev = jnp.sum(parts[:, 1, :], axis=0, keepdims=True) + rows * jnp.sum(
        gaps * gaps, axis=0, keepdims=True
    )
    return mean, lax.rsqrt(dev * (1.0 / (rows * n)) + EPS)


def exchange(spread_rows):
    return lax.all_to_all(spread_rows, AXES, 0, 0, tiled=True)


def first_kernel(x, gain, bias, w_qkv, w_gate, h1, qkv, z1, stats, acc, z):
    i = pl.program_id(0)
    ga, bi = row(gain), row(bias)

    def norm(at):
        n, _ = normed(x[at, :].astype(F32))
        h = (n * ga + bi).astype(BF16)
        h1[at, :] = h
        return h

    def multiply(at, h):
        qkv[at, :] = dot(h, w_qkv[...]).astype(BF16)
        z[at, :] = dot(h, w_gate[...])

    staged(halves_of(x), norm, multiply)
    z1[...] = z[...].astype(BF16)
    add_stats(acc, z[...], i)

    @pl.when(i == pl.num_programs(0) - 1)
    def _():
        spread(acc, stats)


def halves_of(ref):
    step = min(HALF, ref.shape[0] // 2)
    return [slice(j, j + step) for j in range(0, ref.shape[0], step)]


def attend_kernel(flags, qkv, prev, x, gain, bias, w_qkv, out, lse, halo, kvp):
    b = pl.program_id(0)
    width = out.shape[1]
    wide = flags[b] > 0

    @pl.when(wide & (b == 0))
    def _():
        n, _ = normed(x[...].astype(F32))
        h = (n * row(gain) + row(bias)).astype(BF16)
        kvp[...] = dot(h, w_qkv[:, width:]).astype(BF16)
        halo[...] = kvp[...]

    @pl.when(wide & (b > 0))
    def _():
        kvp[...] = prev[:, width:]

    low = lax.broadcasted_iota(jnp.int32, (1, PAIR), 1) < HD
    keys_at = lax.broadcasted_iota(jnp.int32, (SPAN, SPAN), 0)
    allowed = keys_at <= lax.broadcasted_iota(jnp.int32, (SPAN, SPAN), 1)

    def compute(wide):
        turned = {}

        def scores(p, s):
            q_s = pick_head(qkv[:, p * PAIR : (p + 1) * PAIR], s, low) * jnp.asarray(SCALE, BF16)
            at = slice(width + p * PAIR, width + (p + 1) * PAIR)
            res = [jnp.where(allowed, dot_nt(qkv[:, at], q_s), MASKED)]
            if wide:
                res.append(dot_nt(kvp[:, p * PAIR : (p + 1) * PAIR], q_s))
            return res

        def finish(p, s, res):
            if p not in turned:
                v_at = slice(2 * width + p * PAIR, 2 * width + (p + 1) * PAIR)
                turned[p] = [qkv[:, v_at].T]
                if wide:
                    turned[p].append(kvp[:, width + p * PAIR : width + (p + 1) * PAIR].T)
            top = functools.reduce(
                jnp.maximum, [jnp.max(x, axis=0, keepdims=True) for x in res]
            )
            total, acc = 0.0, 0.0
            for x, vt in zip(res, turned[p]):
                e = jnp.exp(x - top)
                total = total + jnp.sum(e, axis=0, keepdims=True)
                acc = acc + dot(vt[s * HD : (s + 1) * HD], e.astype(BF16))
            lse[p, s : s + 1, :] = top + jnp.log(total)
            return acc * (1.0 / total)

        kept = {}

        def end(unit, res):
            p, s = unit
            kept[s] = finish(p, s, res)
            if s == 1:
                both = jnp.concatenate([kept[0], kept[1]], axis=0)
                out[:, p * PAIR : (p + 1) * PAIR] = both.T.astype(BF16)

        in_turn([(p, s) for p in range(width // PAIR) for s in range(2)], lambda u: scores(*u), end)

    pl.when(wide)(functools.partial(compute, True))
    pl.when(jnp.logical_not(wide))(functools.partial(compute, False))


def pick_head(v, s, low):
    return jnp.where(low if s == 0 else ~low, v, jnp.zeros_like(v))


def staged(units, *stages):
    held = [None] * len(units)
    for t in range(len(units) + len(stages) - 1):
        for k, stage in enumerate(stages):
            if 0 <= t - k < len(units):
                u = t - k
                held[u] = stage(units[u]) if k == 0 else stage(units[u], held[u])


def in_turn(units, first, second):
    held = None
    for u in units:
        got = first(u)
        if held is not None:
            second(*held)
        held = (u, got)
    second(*held)


def mix_kernel(
    rows, att, x, z1, parts, gain, shift, ln_gain, ln_bias, w_out, w_gate, y1, h2, z2, stats, acc, st
):
    i = pl.program_id(0)

    @pl.when(i == 0)
    def _():
        mean, rstd = merge_stats(parts, rows)
        st[0:1, :] = mean
        st[1:2, :] = rstd

    mean, rstd = st[0:1, :], st[1:2, :]
    ga, sh, lg, lb = row(gain), row(shift), row(ln_gain), row(ln_bias)

    def project(at):
        return dot(att[at, :], w_out[...])

    def combine(at, branch):
        t = sigmoid((z1[at, :].astype(F32) - mean) * rstd * ga + sh)
        y = t * branch + (1.0 - t) * x[at, :].astype(F32)
        y1[at, :] = y
        n, _ = normed(y)
        h = (n * lg + lb).astype(BF16)
        h2[at, :] = h
        return h

    def gate(at, h):
        z2[at, :] = dot(h, w_gate[...])

    staged(halves_of(att), project, combine, gate)
    add_stats(acc, z2[...], i)

    @pl.when(i == pl.num_programs(0) - 1)
    def _():
        spread(acc, stats)


GELU_C = 0.7978845608028654
GELU_A = 0.044715


def mlp_kernel(h2, w_up, b_up, w_down, b_down, act, slope, mlp):
    units = w_up.shape[1]
    step = 512
    bias, bias_down = row(b_up), row(b_down)

    def up(u):
        rows, j = u
        at = slice(j * step, (j + 1) * step)
        return dot(h2[rows, :], w_up[:, at])

    def curve(u, pre):
        rows, j = u
        at = slice(j * step, (j + 1) * step)
        pre = pre + bias[:, at]
        bend = GELU_C + (GELU_C * GELU_A) * (pre * pre)
        half = 0.5 * jnp.tanh(pre * bend)
        cdf = 0.5 + half
        a = pre * cdf
        act[rows, at] = a.astype(BF16)
        slope[rows, at] = (cdf + a * (0.5 - half) * (6.0 * bend - 4.0 * GELU_C)).astype(BF16)

    def down(u, _):
        rows, j = u
        if j == units // step - 1:
            mlp[rows, :] = dot(act[rows, :], w_down[...]) + bias_down

    staged([(r, j) for r in halves_of(h2) for j in range(units // step)], up, curve, down)


def gate2_kernel(rows, mlp, y1, z2, c, parts, gain, shift, out, dmlp, sums, acc, st):
    i = pl.program_id(0)

    @pl.when(i == 0)
    def _():
        mean, rstd = merge_stats(parts, rows)
        st[0:1, :] = mean
        st[1:2, :] = rstd

    nhat = (z2[...] - st[0:1, :]) * st[1:2, :]
    t = sigmoid(nhat * row(gain) + row(shift))
    m, y = mlp[...], y1[...]
    out[...] = (t * m + (1.0 - t) * y).astype(BF16)
    g = c[...].astype(F32)
    dmlp[...] = (g * t).astype(BF16)
    du = g * (m - y) * t * (1.0 - t)
    add_sums(acc, [column_sum(du), column_sum(du * nhat)], i)

    @pl.when(i == pl.num_programs(0) - 1)
    def _():
        spread(acc, sums)


def mlp_back_kernel(
    core, dmlp, act, slope, h2, w_up, w_down, dh2, keep, send, g_b, acc_up, acc_down
):
    i = pl.program_id(0)

    @pl.when(i == 0)
    def _():
        acc_up[...] = jnp.zeros_like(acc_up)
        acc_down[...] = jnp.zeros_like(acc_down)
        g_b[...] = jnp.zeros_like(g_b)

    d, h = dmlp[...], h2[...]
    units = w_up.shape[1]
    total = 0.0
    width = d.shape[1]
    steps = units // width
    for j in range(steps):
        at = slice(j * width, (j + 1) * width)
        dp = (dot_nt(d, w_down[at, :]) * slope[:, at].astype(F32)).astype(BF16)
        g_b[1 + j : 2 + j, :] += column_sum(dp.astype(F32))
        total = total + dot_nt(dp, w_up[:, at])
        acc_up[at, :] += dot_tn(h, dp)
        acc_down[:, at] += dot_tn(d, act[:, at])
    dh2[...] = total.astype(BF16)
    g_b[0:1, :] += column_sum(d.astype(F32))

    @pl.when(i == pl.num_programs(0) - 1)
    def _():
        for j in range(steps):
            at = slice(j * width, (j + 1) * width)
            half, row0 = (2 * j) // steps, (j % (steps // 2)) * width
            to = slice(row0, row0 + width)
            for out, mine in ((keep, core[0] == half), (send, core[0] != half)):

                @pl.when(mine)
                def _(out=out, at=at, to=to):
                    out[0, to, :] = acc_up[at, :].astype(BF16)
                    out[1, to, :] = acc_down[:, at].T.astype(BF16)


def middle_kernel(
    rows,
    c,
    mlp,
    y1,
    z2,
    dh2p,
    att,
    x,
    z1,
    h2,
    parts2,
    sums2,
    parts1,
    gain2,
    shift2,
    gain1,
    shift1,
    ln_gain,
    g_b,
    w_gate2,
    w_out,
    gx,
    du1,
    datt,
    delta,
    g_w,
    sums,
    g_gate2,
    side,
    acc,
    st,
    acc_gate,
    acc_out,
    dz2,
    dbranch,
):
    i = pl.program_id(0)
    count = 1.0 / (rows * parts2.shape[0])
    width = y1.shape[1]

    @pl.when(i == 0)
    def _():
        mean, rstd = merge_stats(parts2, rows)
        st[0:1, :] = mean
        st[1:2, :] = rstd
        mean, rstd = merge_stats(parts1, rows)
        st[2:3, :] = mean
        st[3:4, :] = rstd
        st[4:5, :] = jnp.sum(sums2[:, 0, :], axis=0, keepdims=True)
        st[5:6, :] = jnp.sum(sums2[:, 1, :], axis=0, keepdims=True)
        g_gate2[...] = st[4:6, :]
        acc_gate[...] = jnp.zeros_like(acc_gate)
        acc_out[...] = jnp.zeros_like(acc_out)

    ga2, sh2, ga1, sh1, lg = row(gain2), row(shift2), row(gain1), row(shift1), row(ln_gain)
    mean2, rstd2, mean1, rstd1 = [st[j : j + 1, :] for j in range(4)]
    shift_mean, gain_mean = st[4:5, :] * count, st[5:6, :] * count
    heads = width // HD
    pick = (
        lax.broadcasted_iota(jnp.int32, (heads, width), 1) // HD
        == lax.broadcasted_iota(jnp.int32, (heads, width), 0)
    ).astype(BF16)
    sums_of = []

    def gate(at):
        g = c[at, :].astype(F32)
        nhat = (z2[at, :] - mean2) * rstd2
        t = sigmoid(nhat * ga2 + sh2)
        rest = g * (1.0 - t)
        du = (rest * t) * (mlp[at, :] - y1[at, :])
        dz2[at, :] = ((ga2 * rstd2) * (du - shift_mean - nhat * gain_mean)).astype(BF16)
        return rest

    def project(at, rest):
        return rest, dot_nt(dz2[at, :], w_gate2[...]), dot(att[at, :], w_out[...])

    def norm(at, held):
        rest, back, branch = held
        dh2 = dh2p[at, :].astype(F32) + back
        n, r = normed(y1[at, :])
        e = dh2 * lg
        dy = rest + r * (
            e - jnp.mean(e, axis=-1, keepdims=True) - n * jnp.mean(e * n, axis=-1, keepdims=True)
        )
        nhat = (z1[at, :].astype(F32) - mean1) * rstd1
        t = sigmoid(nhat * ga1 + sh1)
        dyt = dy * t
        dbranch[at, :] = dyt.astype(BF16)
        out = dy - dyt
        gx[at, :] = out
        du = (out * t) * (branch - x[at, :].astype(F32))
        du1[at, :] = du.astype(BF16)
        sums_of.append(
            [column_sum(du), column_sum(du * nhat), column_sum(dh2 * n), column_sum(dh2)]
        )

    def attended(at, _):
        return dot_nt(dbranch[at, :], w_out[...])

    def finish(at, da):
        da = da.astype(BF16)
        datt[at, :] = da
        prod = da.astype(F32) * att[at, :].astype(F32)
        hi = prod.astype(BF16)
        lo = (prod - hi.astype(F32)).astype(BF16)
        dl = dot_nt(pick, hi) + dot_nt(pick, lo)
        for p in range(heads // 2):
            delta[p, :, at] = dl[2 * p : 2 * p + 2, :]

    staged(halves_of(att), gate, project, norm, attended, finish)
    acc_gate[...] += dot_tn(h2[...], dz2[...])
    acc_out[...] += dot_tn(att[...], dbranch[...])
    add_sums(acc, [sum(v) for v in zip(*sums_of)], i)

    @pl.when(i == pl.num_programs(0) - 1)
    def _():
        spread(acc.at[0:2, :], sums)
        side[0:2, :] = acc[2:4, :]
        side[2:, :] = g_b[...]
        g_w[0] = acc_gate[...].astype(BF16)
        g_w[1] = acc_out[...].astype(BF16)


def back_block(q_ref, k_ref, v_ref, do, lse, delta, kp_ref, vp_ref, wide, own, carry, dq_t):
    width = do.shape[1]
    low = lax.broadcasted_iota(jnp.int32, (1, PAIR), 1) < HD
    mask = lax.broadcasted_iota(jnp.int32, (HALF, HALF), 0) <= lax.broadcasted_iota(
        jnp.int32, (HALF, HALF), 1
    )
    full = slice(0, SPAN)
    parts = [(slice(0, HALF), full), (slice(HALF, SPAN), slice(HALF, SPAN))]
    units = []
    for p in range(width // PAIR):
        for s in range(2):
            units += [(p, s, 0), (p, s, 1)] + ([(p, s, 2)] if wide else [])
    held = {}

    def inputs(p):
        if p not in held:
            held.clear()
            at = slice(p * PAIR, (p + 1) * PAIR)
            q, d, k, v = q_ref[:, at], do[:, at], k_ref[:, at], v_ref[:, at]
            scale = jnp.asarray(SCALE, BF16)
            e = {
                "q": [pick_head(q, s, low) * scale for s in range(2)],
                "do": [pick_head(d, s, low) for s in range(2)],
                "own": (k, v, k.T * scale),
            }
            if wide:
                kp, vp = kp_ref[:, at], vp_ref[:, at]
                e["before"] = (kp, vp, kp.T * scale)
            held[p] = e
        return held[p]

    def first(unit):
        p, s, i = unit
        e = inputs(p)
        ks, qs = (full, full) if i == 2 else parts[i]
        k, v, kt = e["before"] if i == 2 else e["own"]
        q_s, d_s = e["q"][s][qs], e["do"][s][qs]
        kt = kt[s * HD : (s + 1) * HD, ks]
        return dot_nt(k[ks], q_s), dot_nt(v[ks], d_s), q_s, d_s, kt, ks, qs

    def second(unit, got):
        p, s, i = unit
        scores, dp, q_s, d_s, kt, ks, qs = got
        at = slice(p * PAIR, (p + 1) * PAIR)
        x = jnp.exp(scores - lse[p, s : s + 1, qs])
        if i == 0:
            x = jnp.concatenate([jnp.where(mask, x[:, :HALF], 0.0), x[:, HALF:]], axis=1)
        elif i == 1:
            x = jnp.where(mask, x, 0.0)
        ds = (x * (dp - delta[p, s : s + 1, qs])).astype(BF16)
        dk, dv, dq = dot(ds, q_s), dot(x.astype(BF16), d_s), dot(kt, ds)
        target = carry if i == 2 else own
        if s == 0:
            target[0, ks, at] = dk
            target[1, ks, at] = dv
        else:
            target[0, ks, at] += dk
            target[1, ks, at] += dv
        head = slice(p * PAIR + s * HD, p * PAIR + (s + 1) * HD)
        if i == 0:
            dq_t[head, :] = dq
        else:
            dq_t[head, qs] += dq

    in_turn(units, first, second)


def back_first_kernel(flags, q, k, v, do, kp, vp, lse, delta, dq, own, terms, dq_t, carry):
    wide = flags[0] > 0

    @pl.when(wide)
    def _():
        back_block(q, k, v, do, lse, delta, kp, vp, True, own, carry, dq_t)
        terms[...] = carry[...].astype(BF16)

    @pl.when(jnp.logical_not(wide))
    def _():
        back_block(q, k, v, do, lse, delta, kp, vp, False, own, carry, dq_t)
        terms[...] = jnp.zeros_like(terms)

    dq[...] = dq_t[...].T.astype(BF16)


def back_rest_kernel(
    flags, q, k, v, do, kp, vp, lse, delta, dq0, own0, dq, dk, dv, last, dq_t, carry, own
):
    j = pl.program_id(0)
    b = pl.num_programs(0) - 1 - j
    now = lax.rem(j, 2)

    @pl.when(b > 0)
    def _():
        later = carry.at[1 - now]
        wide = flags[b] > 0

        @pl.when(wide)
        def _():
            back_block(q, k, v, do, lse, delta, kp, vp, True, own, later, dq_t)

        @pl.when(jnp.logical_not(wide))
        def _():
            back_block(q, k, v, do, lse, delta, kp, vp, False, own, later, dq_t)
            later[...] = jnp.zeros_like(later)

        @pl.when(j == 0)
        def _():
            last[...] = own[...]

        @pl.when(j > 0)
        def _():
            dk[...] = (own[0] + carry[now, 0]).astype(BF16)
            dv[...] = (own[1] + carry[now, 1]).astype(BF16)

        dq[...] = dq_t[...].T.astype(BF16)

    @pl.when(b == 0)
    def _():
        dq[...] = dq0[...]
        dk[...] = (own0[0] + carry[now, 0]).astype(BF16)
        dv[...] = (own0[1] + carry[now, 1]).astype(BF16)


def last_kernel(
    rows,
    core,
    h1,
    dq_a,
    dk_a,
    dv_a,
    last_a,
    dq_b,
    dk_b,
    dv_b,
    last_b,
    arrived,
    du1,
    z1,
    parts1,
    sums1,
    gain1,
    g_mid,
    side,
    x,
    gx,
    ln_gain,
    w_qkv,
    w_gate1,
    grad_x,
    keep,
    send,
    g_sums,
    acc,
    st,
    dqkv,
    ln_sums,
):
    i = pl.program_id(0)
    final = i == pl.num_programs(0) - 1
    count = 1.0 / (rows * parts1.shape[0])
    width = h1.shape[1]

    @pl.when(i == 0)
    def _():
        mean, rstd = merge_stats(parts1, rows)
        st[2:3, :] = mean
        st[3:4, :] = rstd
        for j in range(sums1.shape[1]):
            g_sums[j : j + 1, :] = jnp.sum(sums1[:, j, :], axis=0, keepdims=True)
        acc[...] = jnp.zeros_like(acc)

    nhat = (z1[...].astype(F32) - st[2:3, :]) * st[3:4, :]
    dz = (
        (row(gain1) * st[3:4, :])
        * (du1[...].astype(F32) - g_sums[0:1, :] * count - nhat * (g_sums[1:2, :] * count))
    ).astype(BF16)

    half = dq_a.shape[1]
    dqkv[:, :half] = dq_a[...]
    dqkv[:, half:width] = dq_b[...]

    @pl.when(jnp.logical_not(final))
    def _():
        dqkv[:, width : width + half] = dk_a[...]
        dqkv[:, width + half : 2 * width] = dk_b[...]
        dqkv[:, 2 * width : 2 * width + half] = dv_a[...]
        dqkv[:, 2 * width + half :] = dv_b[...]

    @pl.when(final)
    def _():
        for j in range(2):
            for c, own in enumerate((last_a, last_b)):
                got = arrived[j, :, c * half : (c + 1) * half].astype(F32)
                at = (1 + j) * width + c * half
                dqkv[:, at : at + half] = (own[j] + got).astype(BF16)

    ht = h1[...].T
    lg = row(ln_gain)
    sums_of = []

    def back(at):
        return dot_nt(dqkv[at, :], w_qkv[...]) + dot_nt(dz[at, :], w_gate1[...])

    def weigh(at, dh):
        for j in range(4):
            if (j >= 2) == (at.start > 0):
                acc[j] += dot(ht, dz if j == 3 else dqkv[:, j * width : (j + 1) * width])
        return dh

    def norm(at, dh):
        n, r = normed(x[at, :].astype(F32))
        e = dh * lg
        grad_x[at, :] = gx[at, :] + r * (
            e - jnp.mean(e, axis=-1, keepdims=True) - n * jnp.mean(e * n, axis=-1, keepdims=True)
        )
        sums_of.append([column_sum(dh * n), column_sum(dh)])

    staged(halves_of(x), back, weigh, norm)
    add_sums(ln_sums, [sum(v) for v in zip(*sums_of)], i)

    @pl.when(final)
    def _():
        mine, other = pl.ds(core[0] * HALF, HALF), pl.ds((1 - core[0]) * HALF, HALF)
        for out, at in ((keep, mine), (send, other)):
            for j in range(4):
                out[j // 2, (j % 2) * HALF : (j % 2 + 1) * HALF, :] = acc[j, at, :].astype(BF16)
            for j in range(2):
                out[j, 2 * HALF : 3 * HALF, :] = g_mid[j, at, :]
                out[j, 3 * HALF :, :] = jnp.zeros((PAD, width), BF16)
        extra = side.shape[0]
        for out, mine in ((keep, core[0] == 0), (send, core[0] != 0)):

            @pl.when(mine)
            def _(out=out):
                out[0, 3 * HALF : 3 * HALF + 16, :] = jnp.concatenate(
                    [ln_sums[...], side[...], jnp.zeros((14 - extra, width), F32)], axis=0
                ).astype(BF16)


def mlp_out_kernel(core, mine, other, g_up, g_down):
    j = pl.program_id(0)
    half = (2 * j) // pl.num_programs(0)
    part = jnp.where(half == core[0], mine[...], other[...]).astype(F32)
    g_up[...] = part[0]
    g_down[...] = part[1]


def rest_out_kernel(core, mine, other, g_qkv, g_gate1, g_out, g_gate2, *vectors):
    width = g_out.shape[1]
    places = (
        ((g_qkv, 0), (g_qkv, 1), (g_gate2, 0)),
        ((g_qkv, 2), (g_gate1, 0), (g_out, 0)),
    )
    for ref, half in ((mine, core[0]), (other, 1 - core[0])):
        at = pl.ds(pl.multiple_of(half * HALF, HALF), HALF)
        for lane, row_places in enumerate(places):
            for j, (out, column) in enumerate(row_places):
                out[at, column * width : (column + 1) * width] = ref[
                    lane, j * HALF : (j + 1) * HALF, :
                ].astype(F32)
    a = mine[0, 3 * HALF : 3 * HALF + 16, :].astype(F32)
    b = other[0, 3 * HALF : 3 * HALF + 16, :].astype(F32)
    extra = jnp.where(core[0] == 0, a, b)
    at = 0
    for out in vectors:
        for j in range(out.shape[0] // width):
            out[j * width : (j + 1) * width] = extra[at]
            at += 1


def between_chips(x):
    seq, head = lax.axis_size("seq"), lax.axis_size("head")
    groups = [[d for d in range(seq * head) if (d // head) % 2 == c] for c in range(2)]
    return lax.all_to_all(x, AXES, 0, 0, axis_index_groups=groups, tiled=True)


def swap(x, axis, bit):
    n = lax.axis_size(axis)
    return lax.ppermute(x, axis, [(i, i ^ bit) for i in range(n)])


def upper(axis, bit):
    return (lax.axis_index(axis) & bit) // bit


def bits(axis):
    return [(axis, 1 << j) for j in range((lax.axis_size(axis) - 1).bit_length())]


class Total:
    def __init__(self, keep, send):
        near = bits("seq")
        first, layer = near[:1], near[1:]
        self.orders = [first + layer, first + layer[::-1]]
        self.far = len(near)
        self.steps = self.far + 1
        self.keep = [keep[0], keep[1]]
        self.send = send
        self.got = None
        self.at = 0

    def _swap(self, parts, stage):
        a, b = self.orders[0][stage], self.orders[1][stage]
        if a == b:
            self.stacked = jnp.stack(parts) if isinstance(parts, list) else parts
            self.both = swap(self.stacked, *a)
            return [self.both[0], self.both[1]]
        return [swap(parts[0], *a), swap(parts[1], *b)]

    def _part(self, lane, start, size):
        a = lax.dynamic_slice_in_dim(self.keep[lane], start, size, 0)
        b = lax.dynamic_slice_in_dim(self.got[lane], start, size, 0)
        return (a.astype(F32) + b.astype(F32)).astype(BF16)

    def left(self):
        return 2 * self.steps - self.at

    def parts(self):
        k, n = self.at, lax.axis_size("head")
        if k == 0:
            return self.send
        rows = self.keep[0].shape[0]
        if k < self.far:
            mine = [upper(*order[k]) for order in self.orders]
            half = rows // 2
            parts = [self._part(lane, (1 - m) * half, half) for lane, m in enumerate(mine)]
            self.keep = [self._part(lane, m * half, half) for lane, m in enumerate(mine)]
            return parts
        place = lax.axis_index("head")
        if k == self.far:
            size = rows // n

            def part(d):
                start = (place ^ d) * size
                return jnp.stack([self._part(lane, start, size) for lane in range(2)])

            parts = [part(d) for d in range(1, n)]
            self.keep = part(0)
            return parts
        if k == self.far + 1:
            total = self.keep.astype(F32)
            for v in self.got:
                total = total + v.astype(F32)
            self.keep = total.astype(BF16)
        elif k == self.far + 2:
            pieces = []
            for j in range(n):
                piece = self.keep
                for d in range(1, n):
                    piece = jnp.where((place ^ j) == d, self.got[d - 1], piece)
                pieces.append(piece)
            joined = jnp.concatenate(pieces, axis=1)
            self.keep = [joined[0], joined[1]]
        else:
            self.keep = self._joined(2 * self.steps - k)
        return self.keep

    def start(self, parts):
        k, n = self.at, lax.axis_size("head")
        if k >= self.steps:
            self.keep = parts
        if self.far <= k <= self.far + 1:
            self.got = [
                swap(parts[d - 1] if k == self.far else parts, "head", d) for d in range(1, n)
            ]
        else:
            self.got = self._swap(parts, k if k < self.far else 2 * self.steps - 1 - k)
        self.at += 1

    def _joined(self, stage):
        out = []
        for lane in range(2):
            up = upper(*self.orders[lane][stage]) > 0
            a, b = self.keep[lane], self.got[lane]
            out.append(jnp.concatenate([jnp.where(up, b, a), jnp.where(up, a, b)], axis=0))
        return out


def arrive_with(total, held):
    total.got, held = lax.optimization_barrier((total.got, held))
    return held


def joint_step(totals, held=()):
    parts, held = lax.optimization_barrier(([t.parts() for t in totals], held))
    for t, p in zip(totals, parts):
        t.start(p)
    return held


def continuation(lengths, span):
    place = jnp.arange(lengths.shape[0], dtype=jnp.int32)
    starts = jnp.sum(jnp.where(place[None, :] < place[:, None], lengths[None, :], 0), axis=1)
    begins = place * span
    hit = (starts[None, :] == begins[:, None]) & (lengths[None, :] > 0)
    return 1 - jnp.max(hit.astype(jnp.int32), axis=1)


def body(
    tokens,
    seq_lengths,
    ln1_gain,
    ln1_bias,
    w_qkv,
    w_out,
    w_gate1,
    gate1_gain,
    gate1_shift,
    ln2_gain,
    ln2_bias,
    w_up,
    b_up,
    w_down,
    b_down,
    w_gate2,
    gate2_gain,
    gate2_shift,
    cotangent,
):
    rows, width = tokens.shape
    units = w_up.shape[1]
    ndev = lax.axis_size("seq") * lax.axis_size("head")
    blocks = rows // SPAN
    pairs = width // PAIR
    heads = width // HD
    count = lax.axis_size("head")
    mac = rows * width * width

    tail = tokens[rows - SPAN :]
    before = lax.ppermute(tail, "head", [(i, i + 1) for i in range(count - 1)])
    flags = lax.dynamic_slice_in_dim(
        continuation(seq_lengths[0], SPAN), lax.axis_index("head") * blocks, blocks, 0
    )

    vec = whole((width,))
    stats_shape = (ndev, 2, width)
    h1, qkv, z1, stats1 = pl.pallas_call(
        first_kernel,
        grid=(rows // TILE,),
        in_specs=[rows_of(width), vec, vec, whole(w_qkv.shape), whole(w_gate1.shape)],
        out_specs=[rows_of(width), rows_of(3 * width), rows_of(width), whole(stats_shape)],
        out_shape=[
            struct((rows, width), BF16),
            struct((rows, 3 * width), BF16),
            struct((rows, width), BF16),
            struct(stats_shape, F32),
        ],
        scratch_shapes=[pltpu.VMEM((2, width), F32), pltpu.VMEM((TILE, width), F32)],
        compiler_params=params(VMEM_MIB),
        cost_estimate=cost(8 * mac, rows * width * 14, rows),
        name="first",
    )(tokens, ln1_gain, ln1_bias, w_qkv, w_gate1)
    parts1 = exchange(stats1)

    att, lse, kv_halo = pl.pallas_call(
        attend_kernel,
        grid_spec=pltpu.PrefetchScalarGridSpec(
            num_scalar_prefetch=1,
            grid=(blocks,),
            in_specs=[
                pl.BlockSpec((SPAN, 3 * width), lambda b, f: (b, 0)),
                pl.BlockSpec((SPAN, 3 * width), lambda b, f: (jnp.maximum(b - 1, 0), 0)),
                whole((SPAN, width)),
                vec,
                vec,
                whole(w_qkv.shape),
            ],
            out_specs=[
                pl.BlockSpec((SPAN, width), lambda b, f: (b, 0)),
                pl.BlockSpec((pairs, 2, SPAN), lambda b, f: (0, 0, b)),
                whole((SPAN, 2 * width)),
            ],
            scratch_shapes=[pltpu.VMEM((SPAN, 2 * width), BF16)],
        ),
        out_shape=[
            struct((rows, width), BF16),
            struct((pairs, 2, rows), F32),
            struct((SPAN, 2 * width), BF16),
        ],
        compiler_params=params(VMEM_MIB),
        cost_estimate=cost(10 * heads * SPAN * SPAN * PAIR * 4, 12 * MIB, heads * SPAN * SPAN * 5),
        name="attend",
    )(flags, qkv, qkv, before, ln1_gain, ln1_bias, w_qkv)

    y1, h2, z2, stats2 = pl.pallas_call(
        functools.partial(mix_kernel, rows),
        grid=(rows // TILE,),
        in_specs=[rows_of(width), rows_of(width), rows_of(width), whole(stats_shape)]
        + [vec] * 4
        + [whole(w_out.shape), whole(w_gate2.shape)],
        out_specs=[rows_of(width), rows_of(width), rows_of(width), whole(stats_shape)],
        out_shape=[
            struct((rows, width), F32),
            struct((rows, width), BF16),
            struct((rows, width), F32),
            struct(stats_shape, F32),
        ],
        scratch_shapes=[pltpu.VMEM((2, width), F32), pltpu.VMEM((8, width), F32)],
        compiler_params=params(VMEM_MIB),
        cost_estimate=cost(4 * mac, rows * width * 18, rows * width),
        name="mix",
    )(att, tokens, z1, parts1, gate1_gain, gate1_shift, ln2_gain, ln2_bias, w_out, w_gate2)
    parts2 = exchange(stats2)

    act, slope, mlp = pl.pallas_call(
        mlp_kernel,
        grid=(blocks,),
        in_specs=[
            rows_of(width, SPAN),
            whole(w_up.shape),
            whole((units,)),
            whole(w_down.shape),
            vec,
        ],
        out_specs=[rows_of(units, SPAN), rows_of(units, SPAN), rows_of(width, SPAN)],
        out_shape=[
            struct((rows, units), BF16),
            struct((rows, units), BF16),
            struct((rows, width), F32),
        ],
        compiler_params=params(VMEM_MIB),
        cost_estimate=cost(4 * rows * width * units, rows * units * 4, rows * units),
        name="mlp",
    )(h2, w_up, b_up, w_down, b_down)

    output, dmlp, sums2 = pl.pallas_call(
        functools.partial(gate2_kernel, rows),
        grid=(rows // TILE,),
        in_specs=[rows_of(width)] * 4 + [whole(stats_shape), vec, vec],
        out_specs=[rows_of(width), rows_of(width), whole(stats_shape)],
        out_shape=[
            struct((rows, width), BF16),
            struct((rows, width), BF16),
            struct(stats_shape, F32),
        ],
        scratch_shapes=[pltpu.VMEM((2, width), F32), pltpu.VMEM((8, width), F32)],
        compiler_params=params(VMEM_MIB),
        cost_estimate=cost(rows * width * 20, rows * width * 18, rows * width),
        name="gate2",
    )(mlp, y1, z2, cotangent, parts2, gate2_gain, gate2_shift)
    parts_du2 = exchange(sums2)

    bias_rows = 1 + units // width
    core = (lax.axis_index("seq") & 1).reshape(1)
    smem = pl.BlockSpec(memory_space=pltpu.SMEM)
    mlp_half = (2, units // 2, width)
    dh2p, keep, send, g_b = pl.pallas_call(
        mlp_back_kernel,
        grid=(blocks,),
        in_specs=[
            smem,
            rows_of(width, SPAN),
            rows_of(units, SPAN),
            rows_of(units, SPAN),
            rows_of(width, SPAN),
            whole(w_up.shape),
            whole(w_down.shape),
        ],
        out_specs=[
            rows_of(width, SPAN),
            whole(mlp_half),
            whole(mlp_half),
            whole((bias_rows, width)),
        ],
        out_shape=[
            struct((rows, width), BF16),
            struct(mlp_half, BF16),
            struct(mlp_half, BF16),
            struct((bias_rows, width), F32),
        ],
        scratch_shapes=[pltpu.VMEM((units, width), F32), pltpu.VMEM((width, units), F32)],
        compiler_params=params(VMEM_MIB),
        cost_estimate=cost(8 * rows * width * units, rows * units * 5),
        name="mlp_back",
    )(core, dmlp, act, slope, h2, w_up, w_down)
    keep, send, dh2p, parts_du2 = lax.optimization_barrier((keep, send, dh2p, parts_du2))
    swapped = swap(send, "seq", 1)
    chips = ndev // 2
    pair_sum = (keep.astype(F32) + swapped.astype(F32)).astype(BF16)
    pair_sum = pair_sum.reshape(chips, units // chips, width)
    pair_sum, dh2p = lax.optimization_barrier((pair_sum, dh2p))
    scattered = between_chips(pair_sum)

    mid_shape = (2, width, width)
    rows_pair = pl.BlockSpec((pairs, 2, MID_TILE), lambda i: (0, 0, i))
    side_rows = 2 + bias_rows
    gx, du1, datt, delta, g_mid, sums1, g_gate2, side = pl.pallas_call(
        functools.partial(middle_kernel, rows),
        grid=(rows // MID_TILE,),
        in_specs=[rows_of(width, MID_TILE)] * 9
        + [whole(stats_shape)] * 3
        + [vec] * 5
        + [whole((bias_rows, width)), whole(w_gate2.shape), whole(w_out.shape)],
        out_specs=[
            rows_of(width, MID_TILE),
            rows_of(width, MID_TILE),
            rows_of(width, MID_TILE),
            rows_pair,
            whole(mid_shape),
            whole(stats_shape),
            whole((2, width)),
            whole((side_rows, width)),
        ],
        out_shape=[
            struct((rows, width), F32),
            struct((rows, width), BF16),
            struct((rows, width), BF16),
            struct((pairs, 2, rows), F32),
            struct(mid_shape, BF16),
            struct(stats_shape, F32),
            struct((2, width), F32),
            struct((side_rows, width), F32),
        ],
        scratch_shapes=[
            pltpu.VMEM((4, width), F32),
            pltpu.VMEM((8, width), F32),
            pltpu.VMEM((width, width), F32),
            pltpu.VMEM((width, width), F32),
            pltpu.VMEM((MID_TILE, width), BF16),
            pltpu.VMEM((MID_TILE, width), BF16),
        ],
        compiler_params=params(VMEM_MIB),
        cost_estimate=cost(10 * mac, rows * width * 38, rows * width * 2),
        name="middle",
    )(
        cotangent,
        mlp,
        y1,
        z2,
        dh2p,
        att,
        tokens,
        z1,
        h2,
        parts2,
        parts_du2,
        parts1,
        gate2_gain,
        gate2_shift,
        gate1_gain,
        gate1_shift,
        ln2_gain,
        g_b,
        w_gate2,
        w_out,
    )

    def columns_at(j, parts=1):
        return lambda i, f: (0, j * parts)

    dq0, own0, terms = pl.pallas_call(
        back_first_kernel,
        grid_spec=pltpu.PrefetchScalarGridSpec(
            num_scalar_prefetch=1,
            grid=(1,),
            in_specs=[
                pl.BlockSpec((SPAN, width), columns_at(0)),
                pl.BlockSpec((SPAN, width), columns_at(1)),
                pl.BlockSpec((SPAN, width), columns_at(2)),
                whole((SPAN, width)),
                pl.BlockSpec((SPAN, width), columns_at(0)),
                pl.BlockSpec((SPAN, width), columns_at(1)),
                whole((pairs, 2, SPAN)),
                whole((pairs, 2, SPAN)),
            ],
            out_specs=[
                whole((SPAN, width)),
                whole((2, SPAN, width)),
                whole((2, SPAN, width)),
            ],
            scratch_shapes=[
                pltpu.VMEM((width, SPAN), F32),
                pltpu.VMEM((2, SPAN, width), F32),
            ],
        ),
        out_shape=[
            struct((SPAN, width), BF16),
            struct((2, SPAN, width), F32),
            struct((2, SPAN, width), BF16),
        ],
        compiler_params=params(VMEM_MIB),
        cost_estimate=cost(
            10 * heads * SPAN * SPAN * PAIR * 2, 8 * MIB, heads * SPAN * SPAN * 2
        ),
        name="attend_back_first",
    )(flags, qkv, qkv, qkv, datt, kv_halo, kv_halo, lse, delta)
    arrived = lax.ppermute(terms, "head", [(i + 1, i) for i in range(count - 1)])

    def block(j):
        return jnp.maximum(blocks - 1 - j, 1)

    groups = 2
    group = width // groups

    def back_rest(g, own0, weight):
        def at(column, shift=0):
            return pl.BlockSpec(
                (SPAN, group), lambda j, f: (block(j) - shift, column * groups + g)
            )

        row_block = pl.BlockSpec((pairs // groups, 2, SPAN), lambda j, f: (g, 0, block(j)))
        out_block = pl.BlockSpec((SPAN, group), lambda j, f: (blocks - 1 - j, 0))
        return pl.pallas_call(
            back_rest_kernel,
            grid_spec=pltpu.PrefetchScalarGridSpec(
                num_scalar_prefetch=1,
                grid=(blocks,),
                in_specs=[
                    at(0),
                    at(1),
                    at(2),
                    at(0),
                    at(1, 1),
                    at(2, 1),
                    row_block,
                    row_block,
                    pl.BlockSpec((SPAN, group), lambda j, f: (0, g)),
                    pl.BlockSpec((2, SPAN, group), lambda j, f: (0, 0, g)),
                ],
                out_specs=[out_block, out_block, out_block, whole((2, SPAN, group))],
                scratch_shapes=[
                    pltpu.VMEM((group, SPAN), F32),
                    pltpu.VMEM((2, 2, SPAN, group), F32),
                    pltpu.VMEM((2, SPAN, group), F32),
                ],
            ),
            out_shape=[struct((rows, group), BF16)] * 3 + [struct((2, SPAN, group), F32)],
            compiler_params=params(VMEM_MIB),
            cost_estimate=cost(
                10 * weight * heads * SPAN * SPAN * PAIR * 3,
                10 * weight * MIB,
                weight * heads * SPAN * SPAN * 2,
            ),
            name="attend_back_rest",
        )(flags, qkv, qkv, qkv, datt, qkv, qkv, lse, delta, dq0, own0)

    back_a = back_rest(0, own0, 1.0)
    back_a, scattered = lax.optimization_barrier((back_a, scattered))
    mine = jnp.sum(scattered.astype(F32), axis=0).astype(BF16)
    mine = jnp.broadcast_to(mine[None], pair_sum.shape)
    mine, own0, sums1 = lax.optimization_barrier((mine, own0, sums1))
    parts_du1 = exchange(sums1)
    back_b = back_rest(1, own0, LATE_WEIGHT)
    mine, parts_du1, back_b, arrived = lax.optimization_barrier((mine, parts_du1, back_b, arrived))
    gathered = between_chips(mine)

    in_half = (2, 3 * HALF + PAD, width)
    grouped = [rows_of(group, SPAN)] * 3 + [whole((2, SPAN, group))]
    grad_x, keep, send, g_sums = pl.pallas_call(
        functools.partial(last_kernel, rows),
        grid=(blocks,),
        in_specs=[smem, rows_of(width, SPAN)]
        + grouped * 2
        + [whole((2, SPAN, width))]
        + [rows_of(width, SPAN)] * 2
        + [whole(stats_shape), whole(stats_shape), vec, whole(mid_shape)]
        + [whole((side_rows, width))]
        + [rows_of(width, SPAN)] * 2
        + [vec, whole(w_qkv.shape), whole(w_gate1.shape)],
        out_specs=[
            rows_of(width, SPAN),
            whole(in_half),
            whole(in_half),
            whole((2, width)),
        ],
        out_shape=[
            struct((rows, width), F32),
            struct(in_half, BF16),
            struct(in_half, BF16),
            struct((2, width), F32),
        ],
        scratch_shapes=[
            pltpu.VMEM((4, width, width), F32),
            pltpu.VMEM((8, width), F32),
            pltpu.VMEM((SPAN, 3 * width), BF16),
            pltpu.VMEM((2, width), F32),
        ],
        compiler_params=params(VMEM_MIB),
        cost_estimate=cost(LATE_WEIGHT * 16 * mac, LATE_WEIGHT * rows * width * 26),
        name="last",
    )(
        core,
        h1,
        *back_a,
        *back_b,
        arrived,
        du1,
        z1,
        parts1,
        parts_du1,
        gate1_gain,
        g_mid,
        side,
        tokens,
        gx,
        ln1_gain,
        w_qkv,
        w_gate1,
    )

    total = Total(keep, send)
    while total.at < total.far:
        joint_step([total])
    gathered = joint_step([total], gathered)
    gathered = gathered.reshape(mlp_half)
    other = swap(gathered, "seq", 1)
    other, gathered = joint_step([total], (other, gathered))
    unit_rows = pl.BlockSpec((2, width, width), lambda j: (0, lax.rem(j, units // width // 2), 0))
    g_up, g_down = pl.pallas_call(
        mlp_out_kernel,
        grid=(units // width,),
        in_specs=[smem, unit_rows, unit_rows],
        out_specs=[
            pl.BlockSpec((width, width), lambda j: (0, j)),
            pl.BlockSpec((width, width), lambda j: (j, 0)),
        ],
        out_shape=[struct(w_up.shape, F32), struct(w_down.shape, F32)],
        compiler_params=params(VMEM_MIB),
        cost_estimate=cost(units * width, 12 * MIB),
        name="mlp_out",
    )(core, gathered, other)
    g_up, g_down = arrive_with(total, (g_up, g_down))
    while total.left():
        joint_step([total])
    vector = struct((width,), F32)
    (
        g_qkv,
        g_gate1,
        g_out,
        g_gate2_w,
        g_ln1_gain,
        g_ln1_bias,
        g_ln2_gain,
        g_ln2_bias,
        g_b_down,
        g_b_up,
    ) = pl.pallas_call(
        rest_out_kernel,
        in_specs=[smem] + [pl.BlockSpec(memory_space=pltpu.VMEM)] * 2,
        out_specs=[pl.BlockSpec(memory_space=pltpu.VMEM)] * 10,
        out_shape=[
            struct(w_qkv.shape, F32),
            struct(w_gate1.shape, F32),
            struct(w_out.shape, F32),
            struct(w_gate2.shape, F32),
        ]
        + [vector] * 5
        + [struct((units,), F32)],
        compiler_params=pltpu.CompilerParams(vmem_limit_bytes=VMEM_MIB * MIB),
        cost_estimate=cost(units * width, 12 * MIB),
        name="rest_out",
    )(core, total.stacked, total.both)
    return (
        output,
        grad_x,
        g_ln1_gain,
        g_ln1_bias,
        g_qkv,
        g_out,
        g_gate1,
        g_sums[1],
        g_sums[0],
        g_ln2_gain,
        g_ln2_bias,
        g_up,
        g_b_up,
        g_down,
        g_b_down,
        g_gate2_w,
        g_gate2[1],
        g_gate2[0],
    )


def solution(mesh):
    split = P(AXES, None)
    return jax.shard_map(
        body,
        mesh=mesh,
        in_specs=(split, P("seq", None)) + (P(),) * 16 + (split,),
        out_specs=(split, split) + (P(),) * 16,
        check_vma=False,
    )
```

```python
import functools

import jax
import jax.numpy as jnp
from jax import lax
from jax.experimental import pallas as pl
from jax.experimental.pallas import tpu as pltpu
from jax.sharding import PartitionSpec as P

HD = 64
SPAN = 512
TILE = 1024
MID_TILE = 512
HALF = 256
PAIR = 128
LATE_WEIGHT = 0.02
EPS = 1e-05
MASKED = -1e30
SCALE = 0.125
AXES = ("seq", "head")
MIB = 1024 * 1024
VMEM_MIB = 60

F32 = jnp.float32
BF16 = jnp.bfloat16


def dot(a, b):
    return jnp.dot(a, b, preferred_element_type=F32)


def dot_nt(a, b):
    return lax.dot_general(a, b, (((1,), (1,)), ((), ())), preferred_element_type=F32)


def dot_tn(a, b):
    return lax.dot_general(a, b, (((0,), (0,)), ((), ())), preferred_element_type=F32)


def struct(shape, dtype):
    return jax.ShapeDtypeStruct(shape, dtype)


def params(mib):
    return pltpu.CompilerParams(vmem_limit_bytes=mib * MIB, dimension_semantics=("arbitrary",))


def cost(flops, nbytes, trans=0):
    return pl.CostEstimate(flops=int(flops), bytes_accessed=int(nbytes), transcendentals=int(trans))


def rows_of(width, tile=TILE):
    return pl.BlockSpec((tile, width), lambda i: (i, 0))


def whole(shape):
    return pl.BlockSpec(shape, lambda *_: (0,) * len(shape))


def normed(v):
    centered = v - jnp.mean(v, axis=-1, keepdims=True)
    rstd = lax.rsqrt(jnp.mean(centered * centered, axis=-1, keepdims=True) + EPS)
    return centered * rstd, rstd


def row(ref):
    return ref[...].reshape(1, -1)


def sigmoid(v):
    return 0.5 + 0.5 * jnp.tanh(0.5 * v)


def column_sum(v):
    return jnp.sum(v, axis=0, keepdims=True)


def add_stats(acc, z, i):
    n = z.shape[0]
    mean = column_sum(z) * (1.0 / n)
    c = z - mean
    dev = column_sum(c * c)

    @pl.when(i == 0)
    def _():
        acc[0:1, :] = mean
        acc[1:2, :] = dev

    @pl.when(i > 0)
    def _():
        before = i.astype(F32)
        gap = mean - acc[0:1, :]
        acc[0:1, :] += gap / (before + 1.0)
        acc[1:2, :] += dev + gap * gap * (n * before / (before + 1.0))


def add_sums(acc, sums, i):
    for j, s in enumerate(sums):

        @pl.when(i == 0)
        def _(j=j, s=s):
            acc[j : j + 1, :] = s

        @pl.when(i > 0)
        def _(j=j, s=s):
            acc[j : j + 1, :] += s


def spread(acc, out):
    out[...] = jnp.broadcast_to(acc[...][None], out.shape)


def merge_stats(parts, rows):
    n = parts.shape[0]
    means = parts[:, 0, :]
    mean = jnp.mean(means, axis=0, keepdims=True)
    gaps = means - mean
    dev = jnp.sum(parts[:, 1, :], axis=0, keepdims=True) + rows * jnp.sum(
        gaps * gaps, axis=0, keepdims=True
    )
    return mean, lax.rsqrt(dev * (1.0 / (rows * n)) + EPS)


def exchange(spread_rows):
    return lax.all_to_all(spread_rows, AXES, 0, 0, tiled=True)


def near(array):
    return pltpu.with_memory_space_constraint(array, pltpu.VMEM)


def first_kernel(x, gain, bias, w_qkv, w_gate, h1, qkv, z1, stats, acc, z):
    i = pl.program_id(0)
    ga, bi = row(gain), row(bias)

    def norm(at):
        n, _ = normed(x[at, :].astype(F32))
        h = (n * ga + bi).astype(BF16)
        h1[at, :] = h
        return h

    def multiply(at, h):
        qkv[at, :] = dot(h, w_qkv[...]).astype(BF16)
        z[at, :] = dot(h, w_gate[...])

    staged(halves_of(x), norm, multiply)
    z1[...] = z[...].astype(BF16)
    add_stats(acc, z[...], i)

    @pl.when(i == pl.num_programs(0) - 1)
    def _():
        spread(acc, stats)


def halves_of(ref):
    step = min(HALF, ref.shape[0] // 2)
    return [slice(j, j + step) for j in range(0, ref.shape[0], step)]


def attend_kernel(flags, qkv, prev, x, gain, bias, w_qkv, out, lse, halo, kvp):
    b = pl.program_id(0)
    width = out.shape[1]
    wide = flags[b] > 0

    @pl.when(wide & (b == 0))
    def _():
        n, _ = normed(x[...].astype(F32))
        h = (n * row(gain) + row(bias)).astype(BF16)
        kvp[...] = dot(h, w_qkv[:, width:]).astype(BF16)
        halo[...] = kvp[...]

    @pl.when(wide & (b > 0))
    def _():
        kvp[...] = prev[:, width:]

    low = lax.broadcasted_iota(jnp.int32, (1, PAIR), 1) < HD
    keys_at = lax.broadcasted_iota(jnp.int32, (SPAN, SPAN), 0)
    allowed = keys_at <= lax.broadcasted_iota(jnp.int32, (SPAN, SPAN), 1)

    def compute(wide):
        turned = {}

        def scores(p, s):
            q_s = pick_head(qkv[:, p * PAIR : (p + 1) * PAIR], s, low) * jnp.asarray(SCALE, BF16)
            at = slice(width + p * PAIR, width + (p + 1) * PAIR)
            res = [jnp.where(allowed, dot_nt(qkv[:, at], q_s), MASKED)]
            if wide:
                res.append(dot_nt(kvp[:, p * PAIR : (p + 1) * PAIR], q_s))
            return res

        def finish(p, s, res):
            if p not in turned:
                v_at = slice(2 * width + p * PAIR, 2 * width + (p + 1) * PAIR)
                turned[p] = [qkv[:, v_at].T]
                if wide:
                    turned[p].append(kvp[:, width + p * PAIR : width + (p + 1) * PAIR].T)
            top = functools.reduce(
                jnp.maximum, [jnp.max(x, axis=0, keepdims=True) for x in res]
            )
            total, acc = 0.0, 0.0
            for x, vt in zip(res, turned[p]):
                e = jnp.exp(x - top)
                total = total + jnp.sum(e, axis=0, keepdims=True)
                acc = acc + dot(vt[s * HD : (s + 1) * HD], e.astype(BF16))
            lse[p, s : s + 1, :] = top + jnp.log(total)
            return acc * (1.0 / total)

        kept = {}

        def end(unit, res):
            p, s = unit
            kept[s] = finish(p, s, res)
            if s == 1:
                both = jnp.concatenate([kept[0], kept[1]], axis=0)
                out[:, p * PAIR : (p + 1) * PAIR] = both.T.astype(BF16)

        in_turn([(p, s) for p in range(width // PAIR) for s in range(2)], lambda u: scores(*u), end)

    pl.when(wide)(functools.partial(compute, True))
    pl.when(jnp.logical_not(wide))(functools.partial(compute, False))


def pick_head(v, s, low):
    return jnp.where(low if s == 0 else ~low, v, jnp.zeros_like(v))


def staged(units, *stages):
    held = [None] * len(units)
    for t in range(len(units) + len(stages) - 1):
        for k, stage in enumerate(stages):
            if 0 <= t - k < len(units):
                u = t - k
                held[u] = stage(units[u]) if k == 0 else stage(units[u], held[u])


def in_turn(units, first, second):
    held = None
    for u in units:
        got = first(u)
        if held is not None:
            second(*held)
        held = (u, got)
    second(*held)


def mix_kernel(
    rows, att, x, z1, parts, gain, shift, ln_gain, ln_bias, w_out, w_gate, y1, h2, z2, stats, acc, st
):
    i = pl.program_id(0)

    @pl.when(i == 0)
    def _():
        mean, rstd = merge_stats(parts, rows)
        st[0:1, :] = mean
        st[1:2, :] = rstd

    mean, rstd = st[0:1, :], st[1:2, :]
    ga, sh, lg, lb = row(gain), row(shift), row(ln_gain), row(ln_bias)

    def project(at):
        return dot(att[at, :], w_out[...])

    def combine(at, branch):
        t = sigmoid((z1[at, :].astype(F32) - mean) * rstd * ga + sh)
        y = t * branch + (1.0 - t) * x[at, :].astype(F32)
        y1[at, :] = y
        n, _ = normed(y)
        h = (n * lg + lb).astype(BF16)
        h2[at, :] = h
        return h

    def gate(at, h):
        z2[at, :] = dot(h, w_gate[...])

    staged(halves_of(att), project, combine, gate)
    add_stats(acc, z2[...], i)

    @pl.when(i == pl.num_programs(0) - 1)
    def _():
        spread(acc, stats)


GELU_C = 0.7978845608028654
GELU_A = 0.044715


def mlp_kernel(h2, w_up, b_up, w_down, b_down, act, slope, mlp):
    units = w_up.shape[1]
    step = 512
    bias, bias_down = row(b_up), row(b_down)

    def up(u):
        rows, j = u
        at = slice(j * step, (j + 1) * step)
        return dot(h2[rows, :], w_up[:, at])

    def curve(u, pre):
        rows, j = u
        at = slice(j * step, (j + 1) * step)
        pre = pre + bias[:, at]
        bend = GELU_C + (GELU_C * GELU_A) * (pre * pre)
        half = 0.5 * jnp.tanh(pre * bend)
        cdf = 0.5 + half
        a = pre * cdf
        act[rows, at] = a.astype(BF16)
        slope[rows, at] = (cdf + a * (0.5 - half) * (6.0 * bend - 4.0 * GELU_C)).astype(BF16)

    def down(u, _):
        rows, j = u
        if j == units // step - 1:
            mlp[rows, :] = dot(act[rows, :], w_down[...]) + bias_down

    staged([(r, j) for r in halves_of(h2) for j in range(units // step)], up, curve, down)


def gate2_kernel(rows, mlp, y1, z2, c, parts, gain, shift, out, dmlp, sums, acc, st):
    i = pl.program_id(0)

    @pl.when(i == 0)
    def _():
        mean, rstd = merge_stats(parts, rows)
        st[0:1, :] = mean
        st[1:2, :] = rstd

    nhat = (z2[...] - st[0:1, :]) * st[1:2, :]
    t = sigmoid(nhat * row(gain) + row(shift))
    m, y = mlp[...], y1[...]
    out[...] = (t * m + (1.0 - t) * y).astype(BF16)
    g = c[...].astype(F32)
    dmlp[...] = (g * t).astype(BF16)
    du = g * (m - y) * t * (1.0 - t)
    add_sums(acc, [column_sum(du), column_sum(du * nhat)], i)

    @pl.when(i == pl.num_programs(0) - 1)
    def _():
        spread(acc, sums)


def mlp_back_kernel(
    core, dmlp, act, slope, h2, w_up, w_down, dh2, keep, send, g_b, acc_up, acc_down
):
    i = pl.program_id(0)

    @pl.when(i == 0)
    def _():
        acc_up[...] = jnp.zeros_like(acc_up)
        acc_down[...] = jnp.zeros_like(acc_down)
        g_b[...] = jnp.zeros_like(g_b)

    d, h = dmlp[...], h2[...]
    units = w_up.shape[1]
    total = 0.0
    width = d.shape[1]
    steps = units // width
    for j in range(steps):
        at = slice(j * width, (j + 1) * width)
        dp = (dot_nt(d, w_down[at, :]) * slope[:, at].astype(F32)).astype(BF16)
        g_b[1 + j : 2 + j, :] += column_sum(dp.astype(F32))
        total = total + dot_nt(dp, w_up[:, at])
        acc_up[at, :] += dot_tn(h, dp)
        acc_down[:, at] += dot_tn(d, act[:, at])
    dh2[...] = total.astype(BF16)
    g_b[0:1, :] += column_sum(d.astype(F32))

    @pl.when(i == pl.num_programs(0) - 1)
    def _():
        for j in range(steps):
            at = slice(j * width, (j + 1) * width)
            half, row0 = (2 * j) // steps, (j % (steps // 2)) * width
            to = slice(row0, row0 + width)
            for out, mine in ((keep, core[0] == half), (send, core[0] != half)):

                @pl.when(mine)
                def _(out=out, at=at, to=to):
                    out[0, to, :] = acc_up[at, :].astype(BF16)
                    out[1, to, :] = acc_down[:, at].T.astype(BF16)


def middle_kernel(
    rows,
    c,
    mlp,
    y1,
    z2,
    dh2p,
    att,
    x,
    z1,
    h2,
    parts2,
    sums2,
    parts1,
    gain2,
    shift2,
    gain1,
    shift1,
    ln_gain,
    g_b,
    w_gate2,
    w_out,
    gx,
    du1,
    datt,
    delta,
    g_w,
    sums,
    g_gate2,
    side,
    acc,
    st,
    acc_gate,
    acc_out,
    dz2,
    dbranch,
):
    i = pl.program_id(0)
    count = 1.0 / (rows * parts2.shape[0])
    width = y1.shape[1]

    @pl.when(i == 0)
    def _():
        mean, rstd = merge_stats(parts2, rows)
        st[0:1, :] = mean
        st[1:2, :] = rstd
        mean, rstd = merge_stats(parts1, rows)
        st[2:3, :] = mean
        st[3:4, :] = rstd
        st[4:5, :] = jnp.sum(sums2[:, 0, :], axis=0, keepdims=True)
        st[5:6, :] = jnp.sum(sums2[:, 1, :], axis=0, keepdims=True)
        g_gate2[...] = st[4:6, :]
        acc_gate[...] = jnp.zeros_like(acc_gate)
        acc_out[...] = jnp.zeros_like(acc_out)

    ga2, sh2, ga1, sh1, lg = row(gain2), row(shift2), row(gain1), row(shift1), row(ln_gain)
    mean2, rstd2, mean1, rstd1 = [st[j : j + 1, :] for j in range(4)]
    shift_mean, gain_mean = st[4:5, :] * count, st[5:6, :] * count
    heads = width // HD
    pick = (
        lax.broadcasted_iota(jnp.int32, (heads, width), 1) // HD
        == lax.broadcasted_iota(jnp.int32, (heads, width), 0)
    ).astype(BF16)
    sums_of = []

    def gate(at):
        g = c[at, :].astype(F32)
        nhat = (z2[at, :] - mean2) * rstd2
        t = sigmoid(nhat * ga2 + sh2)
        rest = g * (1.0 - t)
        du = (rest * t) * (mlp[at, :] - y1[at, :])
        dz2[at, :] = ((ga2 * rstd2) * (du - shift_mean - nhat * gain_mean)).astype(BF16)
        return rest

    def project(at, rest):
        return rest, dot_nt(dz2[at, :], w_gate2[...]), dot(att[at, :], w_out[...])

    def norm(at, held):
        rest, back, branch = held
        dh2 = dh2p[at, :].astype(F32) + back
        n, r = normed(y1[at, :])
        e = dh2 * lg
        dy = rest + r * (
            e - jnp.mean(e, axis=-1, keepdims=True) - n * jnp.mean(e * n, axis=-1, keepdims=True)
        )
        nhat = (z1[at, :].astype(F32) - mean1) * rstd1
        t = sigmoid(nhat * ga1 + sh1)
        dyt = dy * t
        dbranch[at, :] = dyt.astype(BF16)
        out = dy - dyt
        gx[at, :] = out.astype(BF16)
        du = (out * t) * (branch - x[at, :].astype(F32))
        du1[at, :] = du.astype(BF16)
        sums_of.append(
            [column_sum(du), column_sum(du * nhat), column_sum(dh2 * n), column_sum(dh2)]
        )

    def attended(at, _):
        return dot_nt(dbranch[at, :], w_out[...])

    def finish(at, da):
        da = da.astype(BF16)
        datt[at, :] = da
        prod = da.astype(F32) * att[at, :].astype(F32)
        hi = prod.astype(BF16)
        lo = (prod - hi.astype(F32)).astype(BF16)
        dl = dot_nt(pick, hi) + dot_nt(pick, lo)
        for p in range(heads // 2):
            delta[p, :, at] = dl[2 * p : 2 * p + 2, :]

    staged(halves_of(att), gate, project, norm, attended, finish)
    acc_gate[...] += dot_tn(h2[...], dz2[...])
    acc_out[...] += dot_tn(att[...], dbranch[...])
    add_sums(acc, [sum(v) for v in zip(*sums_of)], i)

    @pl.when(i == pl.num_programs(0) - 1)
    def _():
        spread(acc.at[0:2, :], sums)
        side[0:2, :] = acc[2:4, :]
        side[2:, :] = g_b[...]
        g_w[0] = acc_gate[...].astype(BF16)
        g_w[1] = acc_out[...].astype(BF16)


def back_block(q_ref, k_ref, v_ref, do, lse, delta, kp_ref, vp_ref, wide, own, carry, dq_t):
    width = do.shape[1]
    low = lax.broadcasted_iota(jnp.int32, (1, PAIR), 1) < HD
    mask = lax.broadcasted_iota(jnp.int32, (HALF, HALF), 0) <= lax.broadcasted_iota(
        jnp.int32, (HALF, HALF), 1
    )
    full = slice(0, SPAN)
    parts = [(slice(0, HALF), full), (slice(HALF, SPAN), slice(HALF, SPAN))]
    units = []
    for p in range(width // PAIR):
        units += [(p, 0), (p, 1)] + ([(p, 2)] if wide else [])
    held = {}

    def inputs(p):
        if p not in held:
            held.clear()
            at = slice(p * PAIR, (p + 1) * PAIR)
            q, d, k, v = q_ref[:, at], do[:, at], k_ref[:, at], v_ref[:, at]
            scale = jnp.asarray(SCALE, BF16)
            e = {
                "q": [pick_head(q, s, low) * scale for s in range(2)],
                "do": [pick_head(d, s, low) for s in range(2)],
                "own": (k, v, k.T * scale),
            }
            if wide:
                kp, vp = kp_ref[:, at], vp_ref[:, at]
                e["before"] = (kp, vp, kp.T * scale)
            held[p] = e
        return held[p]

    def first(unit):
        p, i = unit
        e = inputs(p)
        ks, qs = (full, full) if i == 2 else parts[i]
        k, v, kt = e["before"] if i == 2 else e["own"]
        q_s, d_s = [q[qs] for q in e["q"]], [d[qs] for d in e["do"]]
        scores = [dot_nt(k[ks], q) for q in q_s]
        dp = [dot_nt(v[ks], d) for d in d_s]
        return scores, dp, q_s, d_s, kt[:, ks], ks, qs

    def second(unit, got):
        p, i = unit
        scores, dp, q_s, d_s, kt, ks, qs = got
        at = slice(p * PAIR, (p + 1) * PAIR)
        low_x, low_ds = [], []
        for s in range(2):
            x = jnp.exp(scores[s] - lse[p, s : s + 1, qs])
            if i == 0:
                x = jnp.concatenate([jnp.where(mask, x[:, :HALF], 0.0), x[:, HALF:]], axis=1)
            elif i == 1:
                x = jnp.where(mask, x, 0.0)
            low_ds.append((x * (dp[s] - delta[p, s : s + 1, qs])).astype(BF16))
            low_x.append(x.astype(BF16))
            dq = dot(kt[s * HD : (s + 1) * HD, :], low_ds[s])
            head = slice(p * PAIR + s * HD, p * PAIR + (s + 1) * HD)
            if i == 0:
                dq_t[head, :] = dq
            else:
                dq_t[head, qs] += dq
        target = carry if i == 2 else own
        target[0, ks, at] = dot(
            jnp.concatenate(low_ds, axis=1), jnp.concatenate(q_s, axis=0)
        )
        target[1, ks, at] = dot(jnp.concatenate(low_x, axis=1), jnp.concatenate(d_s, axis=0))

    in_turn(units, first, second)


def back_first_kernel(flags, q, k, v, do, kp, vp, lse, delta, dq, own, terms, dq_t, carry):
    wide = flags[0] > 0

    @pl.when(wide)
    def _():
        back_block(q, k, v, do, lse, delta, kp, vp, True, own, carry, dq_t)
        terms[...] = carry[...].astype(BF16)

    @pl.when(jnp.logical_not(wide))
    def _():
        back_block(q, k, v, do, lse, delta, kp, vp, False, own, carry, dq_t)
        terms[...] = jnp.zeros_like(terms)

    dq[...] = dq_t[...].T.astype(BF16)


def back_rest_kernel(
    flags, q, k, v, do, kp, vp, lse, delta, dq0, own0, dq, dk, dv, last, dq_t, carry, own
):
    j = pl.program_id(0)
    b = pl.num_programs(0) - 1 - j
    now = lax.rem(j, 2)

    @pl.when(b > 0)
    def _():
        later = carry.at[1 - now]
        wide = flags[b] > 0

        @pl.when(wide)
        def _():
            back_block(q, k, v, do, lse, delta, kp, vp, True, own, later, dq_t)

        @pl.when(jnp.logical_not(wide))
        def _():
            back_block(q, k, v, do, lse, delta, kp, vp, False, own, later, dq_t)
            later[...] = jnp.zeros_like(later)

        @pl.when(j == 0)
        def _():
            last[...] = own[...]

        @pl.when(j > 0)
        def _():
            dk[...] = (own[0] + carry[now, 0]).astype(BF16)
            dv[...] = (own[1] + carry[now, 1]).astype(BF16)

        dq[...] = dq_t[...].T.astype(BF16)

    @pl.when(b == 0)
    def _():
        dq[...] = dq0[...]
        dk[...] = (own0[0] + carry[now, 0]).astype(BF16)
        dv[...] = (own0[1] + carry[now, 1]).astype(BF16)


def last_kernel(
    rows,
    core,
    h1,
    dq_a,
    dk_a,
    dv_a,
    last_a,
    dq_b,
    dk_b,
    dv_b,
    last_b,
    arrived,
    du1,
    z1,
    parts1,
    sums1,
    gain1,
    g_mid,
    side,
    x,
    gx,
    ln_gain,
    w_qkv,
    w_gate1,
    grad_x,
    keep,
    send,
    g_sums,
    acc,
    st,
    dqkv,
    ln_sums,
):
    i = pl.program_id(0)
    final = i == pl.num_programs(0) - 1
    count = 1.0 / (rows * parts1.shape[0])
    width = h1.shape[1]

    @pl.when(i == 0)
    def _():
        mean, rstd = merge_stats(parts1, rows)
        st[2:3, :] = mean
        st[3:4, :] = rstd
        for j in range(sums1.shape[1]):
            g_sums[j : j + 1, :] = jnp.sum(sums1[:, j, :], axis=0, keepdims=True)
        acc[...] = jnp.zeros_like(acc)

    nhat = (z1[...].astype(F32) - st[2:3, :]) * st[3:4, :]
    dz = (
        (row(gain1) * st[3:4, :])
        * (du1[...].astype(F32) - g_sums[0:1, :] * count - nhat * (g_sums[1:2, :] * count))
    ).astype(BF16)

    half = dq_a.shape[1]
    dqkv[:, :half] = dq_a[...]
    dqkv[:, half:width] = dq_b[...]

    @pl.when(jnp.logical_not(final))
    def _():
        dqkv[:, width : width + half] = dk_a[...]
        dqkv[:, width + half : 2 * width] = dk_b[...]
        dqkv[:, 2 * width : 2 * width + half] = dv_a[...]
        dqkv[:, 2 * width + half :] = dv_b[...]

    @pl.when(final)
    def _():
        for j in range(2):
            for c, own in enumerate((last_a, last_b)):
                got = arrived[j, :, c * half : (c + 1) * half].astype(F32)
                at = (1 + j) * width + c * half
                dqkv[:, at : at + half] = (own[j] + got).astype(BF16)

    ht = h1[...].T
    lg = row(ln_gain)
    sums_of = []

    def back(at):
        return dot_nt(dqkv[at, :], w_qkv[...]) + dot_nt(dz[at, :], w_gate1[...])

    def weigh(at, dh):
        for j in range(4):
            if (j >= 2) == (at.start > 0):
                acc[j] += dot(ht, dz if j == 3 else dqkv[:, j * width : (j + 1) * width])
        return dh

    def norm(at, dh):
        n, r = normed(x[at, :].astype(F32))
        e = dh * lg
        grad_x[at, :] = gx[at, :].astype(F32) + r * (
            e - jnp.mean(e, axis=-1, keepdims=True) - n * jnp.mean(e * n, axis=-1, keepdims=True)
        )
        sums_of.append([column_sum(dh * n), column_sum(dh)])

    staged(halves_of(x), back, weigh, norm)
    add_sums(ln_sums, [sum(v) for v in zip(*sums_of)], i)

    @pl.when(final)
    def _():
        mine, other = pl.ds(core[0] * HALF, HALF), pl.ds((1 - core[0]) * HALF, HALF)
        for out, at in ((keep, mine), (send, other)):
            for j in range(4):
                out[j // 2, (j % 2) * HALF : (j % 2 + 1) * HALF, :] = acc[j, at, :].astype(BF16)
            for j in range(2):
                out[j, 2 * HALF : 3 * HALF, :] = g_mid[j, at, :]
                pad = out.shape[1] - 3 * HALF
                out[j, 3 * HALF :, :] = jnp.zeros((pad, width), BF16)
        extra = side.shape[0]
        for out, mine in ((keep, core[0] == 0), (send, core[0] != 0)):

            @pl.when(mine)
            def _(out=out):
                out[0, 3 * HALF : 3 * HALF + 16, :] = jnp.concatenate(
                    [ln_sums[...], side[...], jnp.zeros((14 - extra, width), F32)], axis=0
                ).astype(BF16)


def mlp_out_kernel(core, mine, other, g_up, g_down):
    j = pl.program_id(0)
    half = (2 * j) // pl.num_programs(0)
    part = jnp.where(half == core[0], mine[...], other[...]).astype(F32)
    g_up[...] = part[0]
    g_down[...] = part[1]


def rest_out_kernel(core, mine, other, g_qkv, g_gate1, g_out, g_gate2, *vectors):
    half = pl.program_id(0)
    width = g_out.shape[1]
    places = (
        ((g_qkv, 0), (g_qkv, 1), (g_gate2, 0)),
        ((g_qkv, 2), (g_gate1, 0), (g_out, 0)),
    )

    def write(ref):
        for lane, row_places in enumerate(places):
            for j, (out, column) in enumerate(row_places):
                out[:, column * width : (column + 1) * width] = ref[
                    lane, j * HALF : (j + 1) * HALF, :
                ].astype(F32)

        @pl.when(half == 0)
        def _():
            extra = ref[0, 3 * HALF : 3 * HALF + 16, :].astype(F32)
            at = 0
            for out in vectors:
                for j in range(out.shape[0] // width):
                    out[j * width : (j + 1) * width] = extra[at]
                    at += 1

    pl.when(core[0] == half)(functools.partial(write, mine))
    pl.when(core[0] != half)(functools.partial(write, other))


def between_chips(x):
    seq, head = lax.axis_size("seq"), lax.axis_size("head")
    groups = [[d for d in range(seq * head) if (d // head) % 2 == c] for c in range(2)]
    return lax.all_to_all(x, AXES, 0, 0, axis_index_groups=groups, tiled=True)


def swap(x, axis, bit):
    n = lax.axis_size(axis)
    return lax.ppermute(x, axis, [(i, i ^ bit) for i in range(n)])


def upper(axis, bit):
    return (lax.axis_index(axis) & bit) // bit


def bits(axis):
    return [(axis, 1 << j) for j in range((lax.axis_size(axis) - 1).bit_length())]


class Total:
    def __init__(self, keep, send):
        near = bits("seq")
        first, layer = near[:1], near[1:]
        self.orders = [first + layer, first + layer[::-1]]
        self.far = len(near)
        self.steps = self.far + 1
        self.keep = [keep[0], keep[1]]
        self.send = send
        self.got = None
        self.at = 0

    def _swap(self, parts, stage):
        a, b = self.orders[0][stage], self.orders[1][stage]
        if a == b:
            self.stacked = jnp.stack(parts) if isinstance(parts, list) else parts
            self.both = swap(self.stacked, *a)
            return [self.both[0], self.both[1]]
        return [swap(parts[0], *a), swap(parts[1], *b)]

    def _part(self, lane, start, size):
        a = lax.dynamic_slice_in_dim(self.keep[lane], start, size, 0)
        b = lax.dynamic_slice_in_dim(self.got[lane], start, size, 0)
        return (a.astype(F32) + b.astype(F32)).astype(BF16)

    def left(self):
        return 2 * self.steps - self.at

    def parts(self):
        k, n = self.at, lax.axis_size("head")
        if k == 0:
            return self.send
        rows = self.keep[0].shape[0]
        if k < self.far:
            mine = [upper(*order[k]) for order in self.orders]
            half = rows // 2
            parts = [self._part(lane, (1 - m) * half, half) for lane, m in enumerate(mine)]
            self.keep = [self._part(lane, m * half, half) for lane, m in enumerate(mine)]
            return parts
        place = lax.axis_index("head")
        if k == self.far:
            size = rows // n

            def part(d):
                start = (place ^ d) * size
                return jnp.stack([self._part(lane, start, size) for lane in range(2)])

            parts = [part(d) for d in range(1, n)]
            self.keep = part(0)
            return parts
        if k == self.far + 1:
            total = self.keep.astype(F32)
            for v in self.got:
                total = total + v.astype(F32)
            self.keep = total.astype(BF16)
        elif k == self.far + 2:
            pieces = []
            for j in range(n):
                piece = self.keep
                for d in range(1, n):
                    piece = jnp.where((place ^ j) == d, self.got[d - 1], piece)
                pieces.append(piece)
            joined = jnp.concatenate(pieces, axis=1)
            self.keep = [joined[0], joined[1]]
        else:
            self.keep = self._joined(2 * self.steps - k)
        return self.keep

    def start(self, parts):
        k, n = self.at, lax.axis_size("head")
        if k >= self.steps:
            self.keep = parts
        if self.far <= k <= self.far + 1:
            self.got = [
                swap(parts[d - 1] if k == self.far else parts, "head", d) for d in range(1, n)
            ]
        else:
            self.got = self._swap(parts, k if k < self.far else 2 * self.steps - 1 - k)
        self.at += 1

    def _joined(self, stage):
        out = []
        for lane in range(2):
            up = upper(*self.orders[lane][stage]) > 0
            a, b = self.keep[lane], self.got[lane]
            out.append(jnp.concatenate([jnp.where(up, b, a), jnp.where(up, a, b)], axis=0))
        return out


def arrive_with(total, held):
    total.got, held = lax.optimization_barrier((total.got, held))
    return held


def joint_step(totals, held=()):
    parts, held = lax.optimization_barrier(([t.parts() for t in totals], held))
    for t, p in zip(totals, parts):
        t.start(p)
    return held


def continuation(lengths, span):
    place = jnp.arange(lengths.shape[0], dtype=jnp.int32)
    starts = jnp.sum(jnp.where(place[None, :] < place[:, None], lengths[None, :], 0), axis=1)
    begins = place * span
    hit = (starts[None, :] == begins[:, None]) & (lengths[None, :] > 0)
    return 1 - jnp.max(hit.astype(jnp.int32), axis=1)


def body(
    tokens,
    seq_lengths,
    ln1_gain,
    ln1_bias,
    w_qkv,
    w_out,
    w_gate1,
    gate1_gain,
    gate1_shift,
    ln2_gain,
    ln2_bias,
    w_up,
    b_up,
    w_down,
    b_down,
    w_gate2,
    gate2_gain,
    gate2_shift,
    cotangent,
):
    rows, width = tokens.shape
    units = w_up.shape[1]
    ndev = lax.axis_size("seq") * lax.axis_size("head")
    blocks = rows // SPAN
    pairs = width // PAIR
    heads = width // HD
    count = lax.axis_size("head")
    mac = rows * width * width

    tail = tokens[rows - SPAN :]
    before = lax.ppermute(tail, "head", [(i, i + 1) for i in range(count - 1)])
    flags = lax.dynamic_slice_in_dim(
        continuation(seq_lengths[0], SPAN), lax.axis_index("head") * blocks, blocks, 0
    )

    vec = whole((width,))
    stats_shape = (ndev, 2, width)
    h1, qkv, z1, stats1 = pl.pallas_call(
        first_kernel,
        grid=(rows // TILE,),
        in_specs=[rows_of(width), vec, vec, whole(w_qkv.shape), whole(w_gate1.shape)],
        out_specs=[rows_of(width), rows_of(3 * width), rows_of(width), whole(stats_shape)],
        out_shape=[
            struct((rows, width), BF16),
            struct((rows, 3 * width), BF16),
            struct((rows, width), BF16),
            struct(stats_shape, F32),
        ],
        scratch_shapes=[pltpu.VMEM((2, width), F32), pltpu.VMEM((TILE, width), F32)],
        compiler_params=params(VMEM_MIB),
        cost_estimate=cost(8 * mac, rows * width * 14, rows),
        name="first",
    )(tokens, ln1_gain, ln1_bias, w_qkv, w_gate1)
    parts1 = exchange(stats1)

    att, lse, kv_halo = pl.pallas_call(
        attend_kernel,
        grid_spec=pltpu.PrefetchScalarGridSpec(
            num_scalar_prefetch=1,
            grid=(blocks,),
            in_specs=[
                pl.BlockSpec((SPAN, 3 * width), lambda b, f: (b, 0)),
                pl.BlockSpec((SPAN, 3 * width), lambda b, f: (jnp.maximum(b - 1, 0), 0)),
                whole((SPAN, width)),
                vec,
                vec,
                whole(w_qkv.shape),
            ],
            out_specs=[
                pl.BlockSpec((SPAN, width), lambda b, f: (b, 0)),
                pl.BlockSpec((pairs, 2, SPAN), lambda b, f: (0, 0, b)),
                whole((SPAN, 2 * width)),
            ],
            scratch_shapes=[pltpu.VMEM((SPAN, 2 * width), BF16)],
        ),
        out_shape=[
            struct((rows, width), BF16),
            struct((pairs, 2, rows), F32),
            struct((SPAN, 2 * width), BF16),
        ],
        compiler_params=params(VMEM_MIB),
        cost_estimate=cost(10 * heads * SPAN * SPAN * PAIR * 4, 12 * MIB, heads * SPAN * SPAN * 5),
        name="attend",
    )(flags, qkv, qkv, before, ln1_gain, ln1_bias, w_qkv)

    y1, h2, z2, stats2 = pl.pallas_call(
        functools.partial(mix_kernel, rows),
        grid=(rows // TILE,),
        in_specs=[rows_of(width), rows_of(width), rows_of(width), whole(stats_shape)]
        + [vec] * 4
        + [whole(w_out.shape), whole(w_gate2.shape)],
        out_specs=[rows_of(width), rows_of(width), rows_of(width), whole(stats_shape)],
        out_shape=[
            struct((rows, width), F32),
            struct((rows, width), BF16),
            struct((rows, width), F32),
            struct(stats_shape, F32),
        ],
        scratch_shapes=[pltpu.VMEM((2, width), F32), pltpu.VMEM((8, width), F32)],
        compiler_params=params(VMEM_MIB),
        cost_estimate=cost(4 * mac, rows * width * 18, rows * width),
        name="mix",
    )(att, tokens, z1, near(parts1), gate1_gain, gate1_shift, ln2_gain, ln2_bias, w_out, w_gate2)
    parts2 = exchange(stats2)

    act, slope, mlp = pl.pallas_call(
        mlp_kernel,
        grid=(blocks,),
        in_specs=[
            rows_of(width, SPAN),
            whole(w_up.shape),
            whole((units,)),
            whole(w_down.shape),
            vec,
        ],
        out_specs=[rows_of(units, SPAN), rows_of(units, SPAN), rows_of(width, SPAN)],
        out_shape=[
            struct((rows, units), BF16),
            struct((rows, units), BF16),
            struct((rows, width), F32),
        ],
        compiler_params=params(VMEM_MIB),
        cost_estimate=cost(4 * rows * width * units, rows * units * 4, rows * units),
        name="mlp",
    )(h2, w_up, b_up, w_down, b_down)

    output, dmlp, sums2 = pl.pallas_call(
        functools.partial(gate2_kernel, rows),
        grid=(rows // TILE,),
        in_specs=[rows_of(width)] * 4 + [whole(stats_shape), vec, vec],
        out_specs=[rows_of(width), rows_of(width), whole(stats_shape)],
        out_shape=[
            struct((rows, width), BF16),
            struct((rows, width), BF16),
            struct(stats_shape, F32),
        ],
        scratch_shapes=[pltpu.VMEM((2, width), F32), pltpu.VMEM((8, width), F32)],
        compiler_params=params(VMEM_MIB),
        cost_estimate=cost(rows * width * 20, rows * width * 18, rows * width),
        name="gate2",
    )(mlp, y1, z2, cotangent, near(parts2), gate2_gain, gate2_shift)
    parts_du2 = exchange(sums2)

    bias_rows = 1 + units // width
    core = (lax.axis_index("seq") & 1).reshape(1)
    smem = pl.BlockSpec(memory_space=pltpu.SMEM)
    mlp_half = (2, units // 2, width)
    dh2p, keep, send, g_b = pl.pallas_call(
        mlp_back_kernel,
        grid=(blocks,),
        in_specs=[
            smem,
            rows_of(width, SPAN),
            rows_of(units, SPAN),
            rows_of(units, SPAN),
            rows_of(width, SPAN),
            whole(w_up.shape),
            whole(w_down.shape),
        ],
        out_specs=[
            rows_of(width, SPAN),
            whole(mlp_half),
            whole(mlp_half),
            whole((bias_rows, width)),
        ],
        out_shape=[
            struct((rows, width), BF16),
            pltpu.VMEM(mlp_half, BF16),
            pltpu.VMEM(mlp_half, BF16),
            struct((bias_rows, width), F32),
        ],
        scratch_shapes=[pltpu.VMEM((units, width), F32), pltpu.VMEM((width, units), F32)],
        compiler_params=params(54),
        cost_estimate=cost(8 * rows * width * units, rows * units * 5),
        name="mlp_back",
    )(core, dmlp, act, slope, h2, w_up, w_down)
    keep, send, dh2p, parts_du2 = lax.optimization_barrier((keep, send, dh2p, parts_du2))
    swapped = swap(send, "seq", 1)
    chips = ndev // 2
    pair_sum = (keep.astype(F32) + swapped.astype(F32)).astype(BF16)
    pair_sum = pair_sum.reshape(chips, units // chips, width)
    pair_sum, dh2p = lax.optimization_barrier((pair_sum, dh2p))
    scattered = between_chips(pair_sum)

    mid_shape = (2, width, width)
    rows_pair = pl.BlockSpec((pairs, 2, MID_TILE), lambda i: (0, 0, i))
    side_rows = 2 + bias_rows
    gx, du1, datt, delta, g_mid, sums1, g_gate2, side = pl.pallas_call(
        functools.partial(middle_kernel, rows),
        grid=(rows // MID_TILE,),
        in_specs=[rows_of(width, MID_TILE)] * 9
        + [whole(stats_shape)] * 3
        + [vec] * 5
        + [whole((bias_rows, width)), whole(w_gate2.shape), whole(w_out.shape)],
        out_specs=[
            rows_of(width, MID_TILE),
            rows_of(width, MID_TILE),
            rows_of(width, MID_TILE),
            rows_pair,
            whole(mid_shape),
            whole(stats_shape),
            whole((2, width)),
            whole((side_rows, width)),
        ],
        out_shape=[
            struct((rows, width), BF16),
            struct((rows, width), BF16),
            struct((rows, width), BF16),
            struct((pairs, 2, rows), F32),
            struct(mid_shape, BF16),
            struct(stats_shape, F32),
            struct((2, width), F32),
            struct((side_rows, width), F32),
        ],
        scratch_shapes=[
            pltpu.VMEM((4, width), F32),
            pltpu.VMEM((8, width), F32),
            pltpu.VMEM((width, width), F32),
            pltpu.VMEM((width, width), F32),
            pltpu.VMEM((MID_TILE, width), BF16),
            pltpu.VMEM((MID_TILE, width), BF16),
        ],
        compiler_params=params(VMEM_MIB),
        cost_estimate=cost(10 * mac, rows * width * 38, rows * width * 2),
        name="middle",
    )(
        cotangent,
        mlp,
        y1,
        z2,
        dh2p,
        att,
        tokens,
        z1,
        h2,
        near(parts2),
        near(parts_du2),
        near(parts1),
        gate2_gain,
        gate2_shift,
        gate1_gain,
        gate1_shift,
        ln2_gain,
        g_b,
        w_gate2,
        w_out,
    )

    def columns_at(j, parts=1):
        return lambda i, f: (0, j * parts)

    dq0, own0, terms = pl.pallas_call(
        back_first_kernel,
        grid_spec=pltpu.PrefetchScalarGridSpec(
            num_scalar_prefetch=1,
            grid=(1,),
            in_specs=[
                pl.BlockSpec((SPAN, width), columns_at(0)),
                pl.BlockSpec((SPAN, width), columns_at(1)),
                pl.BlockSpec((SPAN, width), columns_at(2)),
                whole((SPAN, width)),
                pl.BlockSpec((SPAN, width), columns_at(0)),
                pl.BlockSpec((SPAN, width), columns_at(1)),
                whole((pairs, 2, SPAN)),
                whole((pairs, 2, SPAN)),
            ],
            out_specs=[
                whole((SPAN, width)),
                whole((2, SPAN, width)),
                whole((2, SPAN, width)),
            ],
            scratch_shapes=[
                pltpu.VMEM((width, SPAN), F32),
                pltpu.VMEM((2, SPAN, width), F32),
            ],
        ),
        out_shape=[
            struct((SPAN, width), BF16),
            struct((2, SPAN, width), F32),
            struct((2, SPAN, width), BF16),
        ],
        compiler_params=params(VMEM_MIB),
        cost_estimate=cost(
            10 * heads * SPAN * SPAN * PAIR * 2, 8 * MIB, heads * SPAN * SPAN * 2
        ),
        name="attend_back_first",
    )(flags, qkv, qkv, qkv, datt, kv_halo, kv_halo, lse, delta)
    arrived = lax.ppermute(terms, "head", [(i + 1, i) for i in range(count - 1)])

    def block(j):
        return jnp.maximum(blocks - 1 - j, 1)

    groups = 2
    group = width // groups

    def back_rest(g, own0, weight):
        def at(column, shift=0):
            return pl.BlockSpec(
                (SPAN, group), lambda j, f: (block(j) - shift, column * groups + g)
            )

        row_block = pl.BlockSpec((pairs // groups, 2, SPAN), lambda j, f: (g, 0, block(j)))
        out_block = pl.BlockSpec((SPAN, group), lambda j, f: (blocks - 1 - j, 0))
        return pl.pallas_call(
            back_rest_kernel,
            grid_spec=pltpu.PrefetchScalarGridSpec(
                num_scalar_prefetch=1,
                grid=(blocks,),
                in_specs=[
                    at(0),
                    at(1),
                    at(2),
                    at(0),
                    at(1, 1),
                    at(2, 1),
                    row_block,
                    row_block,
                    pl.BlockSpec((SPAN, group), lambda j, f: (0, g)),
                    pl.BlockSpec((2, SPAN, group), lambda j, f: (0, 0, g)),
                ],
                out_specs=[out_block, out_block, out_block, whole((2, SPAN, group))],
                scratch_shapes=[
                    pltpu.VMEM((group, SPAN), F32),
                    pltpu.VMEM((2, 2, SPAN, group), F32),
                    pltpu.VMEM((2, SPAN, group), F32),
                ],
            ),
            out_shape=[struct((rows, group), BF16)] * 3 + [struct((2, SPAN, group), F32)],
            compiler_params=params(VMEM_MIB),
            cost_estimate=cost(
                10 * weight * heads * SPAN * SPAN * PAIR * 3,
                10 * weight * MIB,
                weight * heads * SPAN * SPAN * 2,
            ),
            name="attend_back_rest",
        )(flags, qkv, qkv, qkv, datt, qkv, qkv, lse, delta, dq0, own0)

    back_a = back_rest(0, own0, 1.0)
    back_a, scattered = lax.optimization_barrier((back_a, scattered))
    mine = jnp.sum(scattered.astype(F32), axis=0).astype(BF16)
    mine = jnp.broadcast_to(mine[None], pair_sum.shape)
    mine, own0, sums1 = lax.optimization_barrier((mine, own0, sums1))
    parts_du1 = exchange(sums1)
    back_b = back_rest(1, own0, LATE_WEIGHT)
    mine, parts_du1, back_b, arrived = lax.optimization_barrier((mine, parts_du1, back_b, arrived))
    gathered = between_chips(mine)

    share = 4 * max(ndev // 2, 4)
    in_half = (2, -(-(3 * HALF + 16) // share) * share, width)
    grouped = [rows_of(group, SPAN)] * 3 + [whole((2, SPAN, group))]
    grad_x, keep, send, g_sums = pl.pallas_call(
        functools.partial(last_kernel, rows),
        grid=(blocks,),
        in_specs=[smem, rows_of(width, SPAN)]
        + grouped * 2
        + [whole((2, SPAN, width))]
        + [rows_of(width, SPAN)] * 2
        + [whole(stats_shape), whole(stats_shape), vec, whole(mid_shape)]
        + [whole((side_rows, width))]
        + [rows_of(width, SPAN)] * 2
        + [vec, whole(w_qkv.shape), whole(w_gate1.shape)],
        out_specs=[
            rows_of(width, SPAN),
            whole(in_half),
            whole(in_half),
            whole((2, width)),
        ],
        out_shape=[
            struct((rows, width), F32),
            pltpu.VMEM(in_half, BF16),
            pltpu.VMEM(in_half, BF16),
            struct((2, width), F32),
        ],
        scratch_shapes=[
            pltpu.VMEM((4, width, width), F32),
            pltpu.VMEM((8, width), F32),
            pltpu.VMEM((SPAN, 3 * width), BF16),
            pltpu.VMEM((2, width), F32),
        ],
        compiler_params=params(54),
        cost_estimate=cost(LATE_WEIGHT * 16 * mac, LATE_WEIGHT * rows * width * 26),
        name="last",
    )(
        core,
        h1,
        *back_a,
        *back_b,
        arrived,
        du1,
        z1,
        near(parts1),
        near(parts_du1),
        gate1_gain,
        g_mid,
        side,
        tokens,
        gx,
        ln1_gain,
        w_qkv,
        w_gate1,
    )

    total = Total(keep, send)
    while total.at < total.far:
        joint_step([total])
    gathered = joint_step([total], gathered)
    gathered = gathered.reshape(mlp_half)
    other = swap(gathered, "seq", 1)
    other, gathered = joint_step([total], (other, gathered))
    unit_rows = pl.BlockSpec((2, width, width), lambda j: (0, lax.rem(j, units // width // 2), 0))
    g_up, g_down = pl.pallas_call(
        mlp_out_kernel,
        grid=(units // width,),
        in_specs=[smem, unit_rows, unit_rows],
        out_specs=[
            pl.BlockSpec((width, width), lambda j: (0, j)),
            pl.BlockSpec((width, width), lambda j: (j, 0)),
        ],
        out_shape=[struct(w_up.shape, F32), struct(w_down.shape, F32)],
        compiler_params=params(VMEM_MIB),
        cost_estimate=cost(units * width, 12 * MIB),
        name="mlp_out",
    )(core, gathered, other)
    g_up, g_down = arrive_with(total, (g_up, g_down))
    while total.left():
        joint_step([total])
    vector = struct((width,), F32)
    (
        g_qkv,
        g_gate1,
        g_out,
        g_gate2_w,
        g_ln1_gain,
        g_ln1_bias,
        g_ln2_gain,
        g_ln2_bias,
        g_b_down,
        g_b_up,
    ) = pl.pallas_call(
        rest_out_kernel,
        grid=(2,),
        in_specs=[smem] + [whole(in_half)] * 2,
        out_specs=[pl.BlockSpec((HALF, 3 * width), lambda i: (i, 0))]
        + [pl.BlockSpec((HALF, width), lambda i: (i, 0))] * 3
        + [vec] * 5
        + [whole((units,))],
        out_shape=[
            struct(w_qkv.shape, F32),
            struct(w_gate1.shape, F32),
            struct(w_out.shape, F32),
            struct(w_gate2.shape, F32),
        ]
        + [vector] * 5
        + [struct((units,), F32)],
        compiler_params=params(VMEM_MIB),
        cost_estimate=cost(units * width, 12 * MIB),
        name="rest_out",
    )(core, total.stacked, total.both)
    return (
        output,
        grad_x,
        g_ln1_gain,
        g_ln1_bias,
        g_qkv,
        g_out,
        g_gate1,
        g_sums[1],
        g_sums[0],
        g_ln2_gain,
        g_ln2_bias,
        g_up,
        g_b_up,
        g_down,
        g_b_down,
        g_gate2_w,
        g_gate2[1],
        g_gate2[0],
    )


def solution(mesh):
    split = P(AXES, None)
    return jax.shard_map(
        body,
        mesh=mesh,
        in_specs=(split, P("seq", None)) + (P(),) * 16 + (split,),
        out_specs=(split, split) + (P(),) * 16,
        check_vma=False,
    )
```
